128 devices in a mesh: fsdp: 32 (over x, z, core), rep: 4 (over y).
Axes of the slice: x: 4, y: 4, z: 4, core: 2. Of those that a mesh axis runs over, the one named last changes fastest.
Arguments:
- grads: bfloat16 [64, 1024, 1024], P(None, 'fsdp', 'rep'), may hold values from -1.7 to 1.7
- owner_slot: int32 [64], replicated, may hold values from 0 to 63, each once
- gram_left: float32 [64, 1024, 1024], P('fsdp', 'rep'), may hold values from -1.2 to 1.2
- gram_right: float32 [64, 1024, 1024], P('fsdp', 'rep'), may hold values from -1.2 to 1.2
- root_left: bfloat16 [64, 1024, 1024], P('fsdp', 'rep'), may hold values from -0.6 to 2.6
- root_right: bfloat16 [64, 1024, 1024], P('fsdp'), may hold values from -0.6 to 2.6
- moment: float32 [64, 1024, 1024], P('fsdp', 'rep'), may hold values from -0.18 to 0.18
- second: float32 [64, 1024, 1024], P('fsdp', 'rep'), may hold values from 0.0001 to 0.01
Outputs:
- updates: bfloat16 [64, 1024, 1024], P(None, 'fsdp', 'rep')
- gram_left_new: float32 [64, 1024, 1024], P('fsdp', 'rep')
- gram_right_new: float32 [64, 1024, 1024], P('fsdp', 'rep')
- moment_new: float32 [64, 1024, 1024], P('fsdp', 'rep')
- second_new: float32 [64, 1024, 1024], P('fsdp', 'rep')
The draws below stay inside these ranges and needn't reach their ends.
Inputs may be any that keep to these rules, and one draw needn't show every extreme that they name: `owner_slot`: each slot is named by exactly one block.
All inputs are finite; a program needn't handle non-finite values.
Results may differ from the reference program's by a relative error of at most 0.0049.
Values may be sent and summed in bfloat16 or wider, within the bound.
No kernel may reach another device: no remote copies, remote signals or barrier semaphores. Data moves between devices by JAX's collectives and lax.ppermute only.
A program may use at most 128 MiB of HBM per device.

```python
import math
import jax
import jax.numpy as jnp
from jax import lax

BS = 1024
BLOCKS = 64


def symmetric_root(key, noise):
    diag = jnp.exp(jax.random.uniform(key, (BLOCKS, BS, 1), minval=math.log(0.5), maxval=math.log(2.0)))
    eye_mask = (jnp.arange(BS)[:, None] == jnp.arange(BS)[None, :]).astype(jnp.float32)
    mixed = (noise + jnp.swapaxes(noise, 1, 2)) * (0.35 / math.sqrt(2.0 * BS))
    return (diag * eye_mask + mixed).astype(jnp.bfloat16)


def draw_grads(key, part):
    key = jax.random.fold_in(key, 11)
    key_noise, key_rows, key_cols = jax.random.split(key, 3)
    shape = (BLOCKS, BS, BS)
    row_scale = jnp.exp(jax.random.uniform(key_rows, (BLOCKS, BS, 1), minval=math.log(0.3), maxval=math.log(3.0)))
    col_scale = jnp.exp(jax.random.uniform(key_cols, (BLOCKS, 1, BS), minval=math.log(0.3), maxval=math.log(3.0)))
    noise = jnp.clip(jax.random.normal(key_noise, shape), -5.0, 5.0)
    values = noise * row_scale * col_scale / math.sqrt(BS)
    return jnp.clip(values, -1.69, 1.69).astype(jnp.bfloat16)


def draw_root_left(key, part):
    key = jax.random.fold_in(key, 21)
    key_diag, key_noise = jax.random.split(key)
    noise = jnp.clip(jax.random.normal(key_noise, (BLOCKS, BS, BS)), -5.0, 5.0)
    return symmetric_root(key_diag, noise)


def draw_root_right(key, part):
    key = jax.random.fold_in(key, 31)
    key_diag, key_noise = jax.random.split(key)
    noise = jnp.clip(jax.random.normal(key_noise, (BLOCKS, BS, BS)), -5.0, 5.0)
    return symmetric_root(key_diag, noise)


def levels(stream_key, shape, cuts, low, largest):
    factor_of = 1.0
    for dim, blocks in cuts:
        draws = jax.random.uniform(jax.random.fold_in(jax.random.fold_in(stream_key, 6), dim), (blocks,), jnp.float32, low / len(cuts), largest / len(cuts))
        factor_of = factor_of * jnp.repeat(jnp.exp(draws), shape[dim] // blocks).reshape((-1,) + (1,) * (len(shape) - 1 - dim))
    return factor_of


def gaussian(key, shape, spread, bound, pieces=(), kind=jnp.bfloat16):
    result = jax.random.normal(key, shape, jnp.float32) * spread
    if len(pieces) > 0:
        result = levels(key, shape, pieces, -0.22, 0.18) * result
    return jnp.clip(result, min=-bound, max=bound).astype(kind)


def setup_inputs(seed: int = 0) -> dict:
    splits = jax.random.split(jax.random.key(seed), 9)
    return {
        "grads": draw_grads(jax.random.fold_in(splits[8], 71), 0),
        "owner_slot": jax.random.permutation(splits[1], BLOCKS).astype(jnp.int32),
        "gram_left": gaussian(splits[2], (BLOCKS, BS, BS), 0.2, 1.2, ((0, 32), (1, 4)), jnp.float32),
        "gram_right": gaussian(splits[3], (BLOCKS, BS, BS), 0.2, 1.2, ((0, 32), (1, 4)), jnp.float32),
        "root_left": draw_root_left(jax.random.fold_in(splits[8], 71), 0),
        "root_right": draw_root_right(jax.random.fold_in(splits[8], 71), 0),
        "moment": gaussian(splits[6], (BLOCKS, BS, BS), 0.03, 0.18, ((0, 32), (1, 4)), jnp.float32),
        "second": jnp.clip(jnp.exp(math.log(0.01) - 4.6051702 * jax.random.uniform(splits[7], (BLOCKS, BS, BS), jnp.float32) ** levels(splits[7], (BLOCKS, BS, BS), ((0, 32), (1, 4)), -0.2, 0.2)), 0.0001, 0.01),
    }


def one_slot(items):
    grad, left, right, root_l, root_r, first, secnd = items
    gfloat = grad.astype(jnp.float32)
    left_new = 0.95 * left + 0.05 * jnp.dot(grad, grad.T, preferred_element_type=jnp.float32)
    right_new = 0.95 * right + 0.05 * jnp.dot(grad.T, grad, preferred_element_type=jnp.float32)
    product = jnp.dot(grad, root_r, preferred_element_type=jnp.float32).astype(jnp.bfloat16)
    precond = jnp.dot(root_l, product, preferred_element_type=jnp.float32)
    first_new = 0.9 * first + 0.1 * gfloat
    second_new = 0.95 * secnd + 0.05 * gfloat * gfloat
    adam_dir = first_new / (jnp.sqrt(second_new) + 1e-08)
    ratio = jnp.sqrt(jnp.mean(adam_dir * adam_dir) + 1e-06) / jnp.sqrt(jnp.mean(precond * precond) + 1e-06)
    grafted = (precond * ratio).astype(jnp.bfloat16)
    return (grafted, left_new, right_new, first_new, second_new)

def reference(grads, owner_slot, gram_left, gram_right, root_left, root_right, moment, second):
    blocks = owner_slot.shape[0]
    slot_ids = jnp.arange(blocks, dtype=jnp.int32)
    matches = owner_slot[:, None] == slot_ids[None, :]
    block_of_slot = lax.optimization_barrier(jnp.sum(jnp.where(matches, slot_ids[:, None], 0), axis=0)).astype(jnp.int32)
    slot_grad = grads[block_of_slot]
    grafted, left_new, right_new, first_new, second_new = lax.map(one_slot, (slot_grad, gram_left, gram_right, root_left, root_right, moment, second))
    updates = grafted[owner_slot]
    return (updates, left_new, right_new, first_new, second_new)
```

```python
import functools

import jax
import jax.numpy as jnp
from jax import lax
from jax.experimental import pallas as pl
from jax.experimental.pallas import tpu as pltpu
from jax.sharding import PartitionSpec as P

VMEM_LIMIT = 48 * 1024 * 1024
QUARTERS = 4
PAD = 16
NT = (((1,), (1,)), ((), ()))
TN = (((0,), (0,)), ((), ()))


def params():
    return pltpu.CompilerParams(vmem_limit_bytes=VMEM_LIMIT)


def any_spec():
    return pl.BlockSpec(memory_space=pl.ANY)


def vmem_spec():
    return pl.BlockSpec(memory_space=pltpu.VMEM)


def smem_spec():
    return pl.BlockSpec(memory_space=pltpu.SMEM)


def dot(a, b, dims=(((1,), (0,)), ((), ()))):
    return lax.dot_general(a, b, dims, preferred_element_type=jnp.float32)


def scatter_kernel(slot_ref, grads_ref, even_ref, odd_ref, sem):
    blocks = grads_ref.shape[0]

    def body(b, _):
        slot = slot_ref[b]
        owner = slot // 2

        @pl.when(slot % 2 == 0)
        def _():
            pltpu.make_async_copy(grads_ref.at[b], even_ref.at[owner], sem).start()

        @pl.when(slot % 2 == 1)
        def _():
            pltpu.make_async_copy(grads_ref.at[b], odd_ref.at[owner], sem).start()

        return 0

    lax.fori_loop(0, blocks, body, 0, unroll=8)
    pltpu.make_async_copy(even_ref, even_ref, sem).wait()
    pltpu.make_async_copy(odd_ref, odd_ref, sem).wait()


def scatter(owner_slot, grads):
    blocks, rows, cols = grads.shape
    half = jax.ShapeDtypeStruct((blocks // 2, rows, cols), grads.dtype)
    return pl.pallas_call(
        scatter_kernel,
        out_shape=(half, half),
        in_specs=[smem_spec(), any_spec()],
        out_specs=(any_spec(), any_spec()),
        scratch_shapes=[pltpu.SemaphoreType.DMA],
        compiler_params=params(),
        cost_estimate=pl.CostEstimate(flops=0, bytes_accessed=2 * grads.size * 2, transcendentals=0),
        name="scatter_blocks",
    )(owner_slot, grads)


def gather_kernel(slot_ref, even_ref, odd_ref, out_ref, sem):
    blocks = out_ref.shape[0]

    def body(b, _):
        slot = slot_ref[b]
        owner = slot // 2

        @pl.when(slot % 2 == 0)
        def _():
            pltpu.make_async_copy(even_ref.at[owner], out_ref.at[b], sem).start()

        @pl.when(slot % 2 == 1)
        def _():
            pltpu.make_async_copy(odd_ref.at[owner], out_ref.at[b], sem).start()

        return 0

    lax.fori_loop(0, blocks, body, 0, unroll=8)
    pltpu.make_async_copy(out_ref, out_ref, sem).wait()


def gather(owner_slot, even, odd):
    owners, rows, cols = even.shape
    return pl.pallas_call(
        gather_kernel,
        out_shape=jax.ShapeDtypeStruct((2 * owners, rows, cols), even.dtype),
        in_specs=[smem_spec(), any_spec(), any_spec()],
        out_specs=any_spec(),
        scratch_shapes=[pltpu.SemaphoreType.DMA],
        compiler_params=params(),
        cost_estimate=pl.CostEstimate(flops=0, bytes_accessed=4 * even.size * 2, transcendentals=0),
        name="gather_blocks",
    )(owner_slot, even, odd)


def adam_kernel(rep_ref, g0_ref, g1_ref, g2_ref, g3_ref, mom_ref, sec_ref, *rest):
    mom_out, sec_out, sum_ref = rest[-3:]
    rep = rep_ref[0]
    part = g0_ref.shape[1]
    rows = mom_ref.shape[1]
    total = jnp.zeros((8, part), jnp.float32)
    for j, ref in enumerate((g0_ref, g1_ref, g2_ref, g3_ref)):
        cols = pl.ds(pl.multiple_of(lax.rem(rep + j, QUARTERS) * part, part), part)
        grad = ref[pl.ds(pl.multiple_of(rep * rows, rows), rows), :].astype(jnp.float32)
        first = 0.9 * mom_ref[0, :, cols] + 0.1 * grad
        second = 0.95 * sec_ref[0, :, cols] + 0.05 * grad * grad
        mom_out[0, :, cols] = first
        sec_out[0, :, cols] = second
        way = first / (jnp.sqrt(second) + 1e-08)
        total += jnp.sum((way * way).reshape(rows // 8, 8, part), axis=0)
    sum_ref[...] = total


def adam(k, rep, quarters, moment, second, earlier):
    rows, size = moment.shape[1:]
    part = quarters[0].shape[1]
    out = jax.ShapeDtypeStruct(moment.shape, jnp.float32)
    state = pl.BlockSpec((1, rows, size), lambda i: (k, 0, 0))
    return pl.pallas_call(
        adam_kernel,
        grid=(1,),
        out_shape=(out, out, jax.ShapeDtypeStruct((8, part), jnp.float32)),
        in_specs=[smem_spec()] + [vmem_spec()] * 4 + [state, state] + [any_spec()] * len(earlier),
        out_specs=(state, state, vmem_spec()),
        input_output_aliases={7 + i: i for i in range(len(earlier))},
        compiler_params=params(),
        cost_estimate=pl.CostEstimate(flops=rows * size * 14, bytes_accessed=rows * size * 18, transcendentals=rows * size * 2),
        name="adam_rows",
    )(rep, *quarters, moment, second, *earlier)


def precond_kernel(rep_ref, g0_ref, g1_ref, g2_ref, g3_ref, left_ref, right_ref, adam_ref, out0, out1, out2, out3, acc):
    rep = rep_ref[0]
    part = g0_ref.shape[1]
    rows = left_ref.shape[1]
    left = left_ref[0]
    for j, ref in enumerate((g0_ref, g1_ref, g2_ref, g3_ref)):
        mixed = dot(left, ref[...]).astype(jnp.bfloat16)
        depth = pl.ds(pl.multiple_of(lax.rem(rep + j, QUARTERS) * part, part), part)
        term = dot(mixed, right_ref[0, depth, :])
        if j == 0:
            acc[...] = term
        else:
            acc[...] += term
    whole = acc[...]
    pre_sq = jnp.sum(whole * whole)
    adam_sq = jnp.sum(adam_ref[...])
    pad_row = lax.broadcasted_iota(jnp.int32, (PAD, part), 0)
    pad = jnp.zeros((PAD, part), jnp.float32)
    for first, value in ((0, adam_sq), (3, pre_sq)):
        rest = jnp.full((PAD, part), value, jnp.float32)
        for i in range(3):
            high = rest.astype(jnp.bfloat16).astype(jnp.float32)
            pad = jnp.where(pad_row == first + i, high, pad)
            rest = rest - high
    pad = pad.astype(jnp.bfloat16)
    for j, ref in enumerate((out0, out1, out2, out3)):
        cols = pl.ds(pl.multiple_of(lax.rem(rep + j, QUARTERS) * part, part), part)
        ref[:rows, :] = acc[:, cols].astype(jnp.bfloat16)
        ref[rows:, :] = pad


def precond(k, rep, quarters, root_left, root_right, adam_sq):
    rows, size = root_left.shape[1:]
    part = quarters[0].shape[1]
    piece = jax.ShapeDtypeStruct((rows + PAD, part), jnp.bfloat16)
    return pl.pallas_call(
        precond_kernel,
        grid=(1,),
        out_shape=(piece,) * 4,
        in_specs=[smem_spec()]
        + [vmem_spec()] * 4
        + [
            pl.BlockSpec((1, rows, size), lambda i: (k, 0, 0)),
            pl.BlockSpec((1, size, size), lambda i: (k, 0, 0)),
            vmem_spec(),
        ],
        out_specs=(vmem_spec(),) * 4,
        scratch_shapes=[pltpu.VMEM((rows, size), jnp.float32)],
        compiler_params=params(),
        cost_estimate=pl.CostEstimate(flops=4 * rows * size * size, bytes_accessed=5 * size * size, transcendentals=0),
        name="precond_rows",
    )(rep, *quarters, root_left, root_right, adam_sq)


def gram_kernel(rep_ref, g0_ref, g1_ref, g2_ref, g3_ref, left_ref, right_ref, *rest):
    left_out, right_out = rest[-2:]
    rep = rep_ref[0]
    part = g0_ref.shape[1]
    rows = left_ref.shape[1]
    own = pl.ds(pl.multiple_of(rep * rows, rows), rows)
    for j, ref in enumerate((g0_ref, g1_ref, g2_ref, g3_ref)):
        cols = pl.ds(pl.multiple_of(lax.rem(rep + j, QUARTERS) * part, part), part)
        term = 0.05 * dot(ref[own, :], ref[...], NT)
        if j == 0:
            left_out[0] = 0.95 * left_ref[0] + term
        else:
            left_out[0] += term
        right_out[0, :, cols] = 0.95 * right_ref[0, :, cols] + 0.05 * dot(g0_ref[...], ref[...], TN)


def gram(k, rep, quarters, gram_left, gram_right, earlier):
    rows, size = gram_left.shape[1:]
    out = jax.ShapeDtypeStruct(gram_left.shape, jnp.float32)
    state = pl.BlockSpec((1, rows, size), lambda i: (k, 0, 0))
    return pl.pallas_call(
        gram_kernel,
        grid=(1,),
        out_shape=(out, out),
        in_specs=[smem_spec()] + [vmem_spec()] * 4 + [state, state] + [any_spec()] * len(earlier),
        out_specs=(state, state),
        input_output_aliases={7 + i: i for i in range(len(earlier))},
        compiler_params=params(),
        cost_estimate=pl.CostEstimate(flops=4 * rows * size * size, bytes_accessed=6 * size * size, transcendentals=0),
        name="gram_rows",
    )(rep, *quarters, gram_left, gram_right, *earlier)


def scale_kernel(cells, rep_ref, p0_ref, p1_ref, p2_ref, p3_ref, out_ref):
    rep = rep_ref[0]
    rows = p0_ref.shape[0] - PAD
    sums = jnp.zeros((PAD, p0_ref.shape[1]), jnp.float32)
    pieces = (p0_ref, p1_ref, p2_ref, p3_ref)
    for ref in pieces:
        sums += ref[rows:, :].astype(jnp.float32)
    adam_all = sums[0:1] + sums[1:2] + sums[2:3]
    pre_all = sums[3:4] + sums[4:5] + sums[5:6]
    ratio = jnp.sqrt(adam_all / cells + 1e-06) / jnp.sqrt(pre_all / cells + 1e-06)
    for j, ref in enumerate(pieces):
        where = pl.ds(pl.multiple_of(lax.rem(rep + j, QUARTERS) * rows, rows), rows)
        out_ref[where, :] = (ref[:rows, :].astype(jnp.float32) * ratio).astype(jnp.bfloat16)


def scale(rep, pieces, size):
    rows = pieces[0].shape[0] - PAD
    part = pieces[0].shape[1]
    return pl.pallas_call(
        functools.partial(scale_kernel, float(size * size)),
        out_shape=jax.ShapeDtypeStruct((QUARTERS * rows, part), jnp.bfloat16),
        in_specs=[smem_spec()] + [vmem_spec()] * 4,
        out_specs=vmem_spec(),
        compiler_params=params(),
        cost_estimate=pl.CostEstimate(flops=2 * size * part, bytes_accessed=4 * size * part, transcendentals=0),
        name="scale_rows",
    )(rep, *pieces)


def shift(x, step):
    return lax.ppermute(x, "rep", [(i, (i + step) % QUARTERS) for i in range(QUARTERS)])


def swap(x):
    return lax.all_to_all(x, "fsdp", split_axis=0, concat_axis=0, tiled=True)


def per_device(grads, owner_slot, gram_left, gram_right, root_left, root_right, moment, second):
    row_part, col_part = grads.shape[1:]
    size = root_right.shape[1]
    rep = lax.axis_index("rep").astype(jnp.int32).reshape(1)
    sent = scatter(owner_slot, grads)
    own = [swap(x).reshape(size, col_part) for x in sent]
    before = [shift(x, 1) for x in own]
    after = [shift(x, -1) for x in own]
    across = [shift(before[0], 1), shift(after[1], -1)]
    homed, state, grams = [], (), ()
    for k in range(2):
        quarters = (own[k], after[k], across[k], before[k])
        *state, adam_sq = adam(k, rep, quarters, moment, second, state)
        pieces = precond(k, rep, quarters, root_left, root_right, adam_sq)
        arrived = [pieces[0]] + [shift(pieces[QUARTERS - j], -j) for j in range(1, QUARTERS)]
        grams = gram(k, rep, quarters, gram_left, gram_right, grams)
        scaled = scale(rep, arrived, size)
        homed.append(swap(scaled.reshape(-1, row_part, col_part)))
    updates = gather(owner_slot, *homed)
    return (updates, *grams, *state)


def solution(mesh):
    return jax.shard_map(
        per_device,
        mesh=mesh,
        in_specs=(
            P(None, "fsdp", "rep"),
            P(),
            P("fsdp", "rep", None),
            P("fsdp", "rep", None),
            P("fsdp", "rep", None),
            P("fsdp", None, None),
            P("fsdp", "rep", None),
            P("fsdp", "rep", None),
        ),
        out_specs=(
            P(None, "fsdp", "rep"),
            P("fsdp", "rep", None),
            P("fsdp", "rep", None),
            P("fsdp", "rep", None),
            P("fsdp", "rep", None),
        ),
        check_vma=False,
    )
```

```python
import functools

import jax
import jax.numpy as jnp
from jax import lax
from jax.experimental import pallas as pl
from jax.experimental.pallas import tpu as pltpu
from jax.sharding import PartitionSpec as P

VMEM_LIMIT = 32 * 1024 * 1024
REPS = 4
OWNERS = 32
LANES = 128
NN = (((1,), (0,)), ((), ()))
NT = (((1,), (1,)), ((), ()))
TN = (((0,), (0,)), ((), ()))
ANY = pl.BlockSpec(memory_space=pl.ANY)
VMEM = pl.BlockSpec(memory_space=pltpu.VMEM)
SMEM = pl.BlockSpec(memory_space=pltpu.SMEM)
BF16 = jnp.bfloat16
F32 = jnp.float32


def params():
    return pltpu.CompilerParams(vmem_limit_bytes=VMEM_LIMIT)


def cost(flops, nbytes):
    return pl.CostEstimate(flops=flops, bytes_accessed=nbytes, transcendentals=0)


def dot(a, b, dims=NN):
    return lax.dot_general(a, b, dims, preferred_element_type=F32)


def shape(dims, dtype):
    return jax.ShapeDtypeStruct(dims, dtype)


def place():
    rep = lax.axis_index("rep").astype(jnp.int32)
    core = lax.rem(lax.axis_index("fsdp").astype(jnp.int32), 2)
    return jnp.stack([rep, lax.rem(rep, 2), lax.rem(rep + 1 - 2 * core + REPS, REPS)])


def to_neighbour(x):
    pairs = []
    for owner in range(OWNERS):
        step = 1 - 2 * (owner % 2)
        for rep in range(REPS):
            pairs.append((owner * REPS + rep, owner * REPS + (rep + step) % REPS))
    return lax.ppermute(x, ("fsdp", "rep"), pairs)


def shift(x, step):
    return lax.ppermute(x, "rep", [(i, (i + step) % REPS) for i in range(REPS)])


def everyone(x):
    return lax.all_to_all(x, ("fsdp", "rep"), split_axis=0, concat_axis=0, tiled=True)


def scatter_kernel(slot_ref, grads_ref, out_ref, sem):
    def body(b, _):
        slot = slot_ref[b]
        first = (slot // 2) * REPS + lax.rem(slot, 2)
        pltpu.make_async_copy(grads_ref.at[b], out_ref.at[first], sem).start()
        pltpu.make_async_copy(grads_ref.at[b], out_ref.at[first + 2], sem).start()
        return 0

    lax.fori_loop(0, grads_ref.shape[0], body, 0, unroll=8)
    pltpu.make_async_copy(out_ref, out_ref, sem).wait()


def scatter(owner_slot, grads):
    blocks, rows, cols = grads.shape
    return pl.pallas_call(
        scatter_kernel,
        out_shape=shape((2 * blocks, rows, cols), grads.dtype),
        in_specs=[SMEM, ANY],
        out_specs=ANY,
        scratch_shapes=[pltpu.SemaphoreType.DMA],
        compiler_params=params(),
        cost_estimate=cost(0, 6 * grads.size),
        name="scatter_blocks",
    )(owner_slot, grads)


def precond_kernel(at_ref, g_ref, l0_ref, l1_ref, l2_ref, l3_ref, right_ref, out_ref, sum_ref, left, mixed):
    rep = at_ref[0]
    owners, reps, row_part, part = g_ref.shape
    size = owners * row_part
    share = l0_ref.shape[0] * l0_ref.shape[1]
    for j, ref in enumerate((l0_ref, l1_ref, l2_ref, l3_ref)):
        first = lax.rem(rep - j + REPS, REPS) * share
        left[pl.ds(pl.multiple_of(first, share), share), :] = ref[...].reshape(share, size)
    for j in range(reps):
        column = g_ref[:, j].reshape(size, part)
        mixed[:, j * part : (j + 1) * part] = dot(left[...], column).astype(BF16)
    total = jnp.zeros((8, part), F32)
    for j in range(reps):
        piece = dot(mixed[...], right_ref[0, :, j * part : (j + 1) * part])
        total += jnp.sum((piece * piece).reshape(-1, 8, part), axis=0)
        out_ref[:, j, :, :part] = piece.astype(BF16).reshape(owners, -1, part)
    sum_ref[...] = total


def precond(at, arrived, left_parts, root_right):
    owners, reps, row_part, part = arrived.shape
    size = root_right.shape[1]
    half = row_part // 2
    return pl.pallas_call(
        precond_kernel,
        grid_spec=pltpu.PrefetchScalarGridSpec(
            num_scalar_prefetch=1,
            grid=(1,),
            in_specs=[VMEM] * 5 + [pl.BlockSpec((1, size, size), lambda i, at: (at[1], 0, 0))],
            out_specs=(VMEM, VMEM),
            scratch_shapes=[pltpu.VMEM((owners * half, size), BF16), pltpu.VMEM((owners * half, size), BF16)],
        ),
        out_shape=(shape((owners, reps, half, part + LANES), BF16), shape((8, part), F32)),
        compiler_params=params(),
        cost_estimate=cost(2 * size**3, 7 * size * size),
        name="precond_rows",
    )(at, arrived, *left_parts, root_right)


def adam_kernel(at_ref, own_ref, other_ref, mom_ref, sec_ref, pre_ref, _, mom_out, sec_out, out_ref, sums, pads, sem):
    which, step = pl.program_id(0), pl.program_id(1)
    chunk, reps, row_part, part = own_ref.shape
    rows = chunk * row_part

    @pl.when((which == 0) & (step == 0))
    def _():
        sums[...] = jnp.zeros_like(sums)

    def work(ref, i):
        total = jnp.zeros((8, part), F32)
        for j in range(reps):
            cols = slice(j * part, (j + 1) * part)
            grad = ref[:, j].reshape(rows, part).astype(F32)
            first = 0.9 * mom_ref[0, :, cols] + 0.1 * grad
            second = 0.95 * sec_ref[0, :, cols] + 0.05 * grad * grad
            mom_out[0, :, cols] = first
            sec_out[0, :, cols] = second
            way = first / (jnp.sqrt(second) + 1e-08)
            total += jnp.sum((way * way).reshape(rows // 8, 8, part), axis=0)
        sums[i] += total

    @pl.when(which == 0)
    def _():
        work(own_ref, 0)

    @pl.when(which == 1)
    def _():
        work(other_ref, 1)

    @pl.when((which == 1) & (step == pl.num_programs(1) - 1))
    def _():
        own, other = jnp.sum(sums[0]), jnp.sum(sums[1])
        even = at_ref[1] == 0
        values = (jnp.where(even, own, other), jnp.where(even, other, own), jnp.sum(pre_ref[...]))
        tile = pads.shape[2:]
        row = lax.broadcasted_iota(jnp.int32, tile, 0)
        pad = jnp.zeros(tile, F32)
        for i, value in enumerate(values):
            rest = jnp.full(tile, value, F32)
            for n in range(3):
                high = rest.astype(BF16).astype(F32)
                pad = jnp.where(row == 3 * i + n, high, pad)
                rest = rest - high
        pads[...] = jnp.broadcast_to(pad.astype(BF16), pads.shape)
        copy = pltpu.make_async_copy(pads, out_ref.at[:, :, :, pl.ds(part, LANES)], sem)
        copy.start()
        copy.wait()


def adam(at, arrived, other, moment, second, pre_sq, pieces, steps=4):
    owners, reps, row_part, part = arrived.shape
    _, rows, size = moment.shape
    chunk = other.shape[0] // steps
    state = pl.BlockSpec(
        (1, rows // steps, size), lambda i, n, at: (lax.rem(at[1] + i, 2), n, 0)
    )
    own_spec = pl.BlockSpec(
        (chunk, reps, row_part, part), lambda i, n, at: (at[0] * steps + jnp.where(i == 0, n, steps - 1), 0, 0, 0)
    )
    other_spec = pl.BlockSpec((chunk, reps, row_part, part), lambda i, n, at: (jnp.where(i == 0, 0, n), 0, 0, 0))
    return pl.pallas_call(
        adam_kernel,
        grid_spec=pltpu.PrefetchScalarGridSpec(
            num_scalar_prefetch=1,
            grid=(2, steps),
            in_specs=[own_spec, other_spec, state, state, VMEM, ANY],
            out_specs=(state, state, ANY),
            scratch_shapes=[
                pltpu.VMEM((2, 8, part), F32),
                pltpu.VMEM(pieces.shape[:3] + (LANES,), BF16),
                pltpu.SemaphoreType.DMA,
            ],
        ),
        out_shape=(shape(moment.shape, F32), shape(second.shape, F32), shape(pieces.shape, BF16)),
        input_output_aliases={6: 2},
        compiler_params=params(),
        cost_estimate=cost(30 * rows * size, 40 * rows * size),
        name="adam_rows",
    )(at, arrived, other, moment, second, pre_sq, pieces)


def left_kernel(at_ref, g_ref, stat_ref, new_ref, part_ref, whole, lhs):
    owners, reps, row_part, part = g_ref.shape
    size = owners * row_part
    rows = stat_ref.shape[1]
    blocks = rows // row_part
    for j in range(reps):
        cols = slice(j * part, (j + 1) * part)
        whole[:, cols] = g_ref[:, j].reshape(size, part)
        for i, index in enumerate((at_ref[0], at_ref[2])):
            lhs[i * rows : (i + 1) * rows, cols] = g_ref[pl.ds(index * blocks, blocks), j].reshape(rows, part)
    for j in range(reps):
        cols = slice(j * part, (j + 1) * part)
        term = 0.05 * dot(lhs[...], whole[cols, :], NT)
        new_ref[0, :, cols] = 0.95 * stat_ref[0, :, cols] + term[:rows]
        part_ref[:, cols] = term[rows:].astype(BF16)


def right_kernel(at_ref, g_ref, stat_ref, new_ref, part_ref, lhs):
    owners, reps, row_part, part = g_ref.shape
    size = owners * row_part
    rows = stat_ref.shape[1]
    for i, index in enumerate((at_ref[0], at_ref[2])):
        lhs[:, i * rows : (i + 1) * rows] = g_ref[:, pl.ds(index, 1)].reshape(size, part)
    for j in range(reps):
        cols = slice(j * part, (j + 1) * part)
        term = 0.05 * dot(lhs[...], g_ref[:, j].reshape(size, part), TN)
        new_ref[0, :, cols] = 0.95 * stat_ref[0, :, cols] + term[:rows]
        part_ref[:, cols] = term[rows:].astype(BF16)


def gram(kernel, scratch, at, arrived, stat):
    _, rows, size = stat.shape
    state = pl.BlockSpec((1, rows, size), lambda i, at: (at[1], 0, 0))
    return pl.pallas_call(
        kernel,
        grid_spec=pltpu.PrefetchScalarGridSpec(
            num_scalar_prefetch=1,
            grid=(1,),
            in_specs=[VMEM, state],
            out_specs=(state, VMEM),
            scratch_shapes=scratch,
        ),
        out_shape=(shape(stat.shape, F32), shape((rows, size), BF16)),
        compiler_params=params(),
        cost_estimate=cost(4 * rows * size * size, 12 * rows * size + 2 * size * size),
        name=kernel.__name__,
    )(at, arrived, stat)


def add_kernel(at_ref, left_part, right_part, left_ref, right_ref, _, __, left_out, right_out):
    left_out[0] = 0.95 * left_ref[0] + left_part[...].astype(F32)
    right_out[0] = 0.95 * right_ref[0] + right_part[...].astype(F32)


def add(at, left_part, right_part, gram_left, gram_right, left_new, right_new, steps=4):
    _, rows, size = gram_left.shape
    state = pl.BlockSpec((1, rows // steps, size), lambda n, at: (1 - at[1], n, 0))
    term = pl.BlockSpec((rows // steps, size), lambda n, at: (n, 0))
    return pl.pallas_call(
        add_kernel,
        grid_spec=pltpu.PrefetchScalarGridSpec(
            num_scalar_prefetch=1,
            grid=(steps,),
            in_specs=[term, term, state, state, ANY, ANY],
            out_specs=(state, state),
        ),
        out_shape=(shape(gram_left.shape, F32), shape(gram_right.shape, F32)),
        input_output_aliases={5: 0, 6: 1},
        compiler_params=params(),
        cost_estimate=cost(4 * rows * size, 20 * rows * size),
        name="add_terms",
    )(at, left_part, right_part, gram_left, gram_right, left_new, right_new)


def finish_kernel(cells, slot_ref, in_ref, out_ref, ratios):
    owners = in_ref.shape[0] // REPS
    half = in_ref.shape[1]
    part = in_ref.shape[2] - LANES

    def ratio(owner, _):
        sums = in_ref[pl.ds(owner * REPS, REPS), :, part:].astype(F32)
        adam_sums = jnp.sum(sums, axis=0)
        for k in range(2):
            pre_sums = sums[k] + sums[k + 2]
            adam_all = adam_sums[3 * k : 3 * k + 1] + adam_sums[3 * k + 1 : 3 * k + 2] + adam_sums[3 * k + 2 : 3 * k + 3]
            pre_all = pre_sums[6:7] + pre_sums[7:8] + pre_sums[8:9]
            value = jnp.sqrt(adam_all / cells + 1e-06) / jnp.sqrt(pre_all / cells + 1e-06)
            ratios[2 * owner + k] = jnp.broadcast_to(value, ratios.shape[1:])
        return 0

    lax.fori_loop(0, owners, ratio, 0, unroll=4)

    def place_block(b, _):
        slot = slot_ref[b]
        first = (slot // 2) * REPS + lax.rem(slot, 2)
        by = ratios[slot]
        by = jnp.concatenate([by] * (half // by.shape[0]), axis=0)
        by = jnp.concatenate([by] * (part // LANES), axis=1)
        for n in range(2):
            piece = in_ref[first + 2 * n, :, :part].astype(F32) * by
            out_ref[b, n * half : (n + 1) * half, :] = piece.astype(BF16)
        return 0

    lax.fori_loop(0, out_ref.shape[0], place_block, 0, unroll=4)


def finish(owner_slot, pieces, size):
    count, half, wide = pieces.shape
    blocks = owner_slot.shape[0]
    part = wide - LANES
    return pl.pallas_call(
        functools.partial(finish_kernel, float(size * size)),
        out_shape=shape((blocks, 2 * half, part), BF16),
        in_specs=[SMEM, VMEM],
        out_specs=VMEM,
        scratch_shapes=[pltpu.VMEM((blocks, 8, LANES), F32)],
        compiler_params=params(),
        cost_estimate=cost(4 * blocks * half * part, 10 * blocks * half * part),
        name="finish_updates",
    )(owner_slot, pieces)


def per_device(grads, owner_slot, gram_left, gram_right, root_left, root_right, moment, second):
    blocks, row_part, part = grads.shape
    _, rows, size = root_left.shape
    at = place()
    arrived = everyone(scatter(owner_slot, grads)).reshape(OWNERS, REPS, row_part, part)

    dealt = root_left.reshape(2, rows // row_part, 2, row_part // 2, size)
    dealt = jnp.transpose(dealt, (2, 0, 1, 3, 4)).reshape(REPS, rows // row_part, row_part // 2, size)
    own_parts = [
        lax.dynamic_index_in_dim(dealt, lax.rem(at[0] + j, REPS), 0, keepdims=False) for j in range(REPS)
    ]
    left_parts = own_parts[:1] + [shift(own_parts[j], j) for j in range(1, REPS)]

    count = rows // row_part
    other = to_neighbour(lax.dynamic_slice_in_dim(arrived, at[2] * count, count, 0))
    pieces, pre_sq = precond(at, arrived, left_parts, root_right)
    left_new, left_term = gram(
        left_kernel,
        [pltpu.VMEM((size, size), BF16), pltpu.VMEM((2 * rows, size), BF16)],
        at,
        arrived,
        gram_left,
    )
    left_term = to_neighbour(left_term)
    moment_new, second_new, pieces = adam(at, arrived, other, moment, second, pre_sq, pieces)
    homed = everyone(pieces.reshape(OWNERS * REPS, row_part // 2, part + LANES))
    right_new, right_term = gram(
        right_kernel, [pltpu.VMEM((size, 2 * rows), BF16)], at, arrived, gram_right
    )
    right_term = to_neighbour(right_term)
    left_new, right_new = add(at, left_term, right_term, gram_left, gram_right, left_new, right_new)
    updates = finish(owner_slot, homed, size)
    return (updates, left_new, right_new, moment_new, second_new)


def solution(mesh):
    return jax.shard_map(
        per_device,
        mesh=mesh,
        in_specs=(
            P(None, "fsdp", "rep"),
            P(),
            P("fsdp", "rep", None),
            P("fsdp", "rep", None),
            P("fsdp", "rep", None),
            P("fsdp", None, None),
            P("fsdp", "rep", None),
            P("fsdp", "rep", None),
        ),
        out_specs=(
            P(None, "fsdp", "rep"),
            P("fsdp", "rep", None),
            P("fsdp", "rep", None),
            P("fsdp", "rep", None),
            P("fsdp", "rep", None),
        ),
        check_vma=False,
    )
```

```python
import functools

import jax
import jax.numpy as jnp
from jax import lax
from jax.experimental import pallas as pl
from jax.experimental.pallas import tpu as pltpu
from jax.sharding import PartitionSpec as P

VMEM_LIMIT = 32 * 1024 * 1024
MID_LIMIT = 60 * 1024 * 1024
LATE_LIMIT = 60 * 1024 * 1024
REPS = 4
OWNERS = 32
LANES = 128
NN = (((1,), (0,)), ((), ()))
NT = (((1,), (1,)), ((), ()))
TN = (((0,), (0,)), ((), ()))
ANY = pl.BlockSpec(memory_space=pl.ANY)
VMEM = pl.BlockSpec(memory_space=pltpu.VMEM)
SMEM = pl.BlockSpec(memory_space=pltpu.SMEM)
BF16 = jnp.bfloat16
F32 = jnp.float32


def params(limit=VMEM_LIMIT):
    return pltpu.CompilerParams(vmem_limit_bytes=limit)


def cost(flops, nbytes):
    return pl.CostEstimate(flops=flops, bytes_accessed=nbytes, transcendentals=0)


def dot(a, b, dims=NN):
    return lax.dot_general(a, b, dims, preferred_element_type=F32)


def shape(dims, dtype):
    return jax.ShapeDtypeStruct(dims, dtype)


GRAM_COST = cost(1, 1)
MID_COST = cost(10**11, 10**6)


def place():
    rep = lax.axis_index("rep").astype(jnp.int32)
    core = lax.rem(lax.axis_index("fsdp").astype(jnp.int32), 2)
    step = 1 - 2 * core
    return jnp.stack([rep, lax.rem(rep, 2), lax.rem(rep + step + REPS, REPS), step])


def to_neighbour(x, far=1):
    pairs = []
    for owner in range(OWNERS):
        step = far * (1 - 2 * (owner % 2))
        for rep in range(REPS):
            pairs.append((owner * REPS + rep, owner * REPS + (rep + step) % REPS))
    return lax.ppermute(x, ("fsdp", "rep"), pairs)


def everyone(x):
    return lax.all_to_all(x, ("fsdp", "rep"), split_axis=0, concat_axis=0, tiled=True)


def deal_kernel(at_ref, slot_ref, grads_ref, left_ref, out_ref, keep_ref, ahead_ref, across_ref, back_ref):
    def share(j):
        to = lax.rem(at_ref[0] + j * at_ref[3] + REPS, REPS)
        return left_ref[lax.rem(to, 2), :, to // 2]

    keep_ref[...] = share(0)
    ahead_ref[...] = share(1)
    across_ref[...] = share(2)
    back_ref[...] = share(-1)

    def body(b, _):
        slot = slot_ref[b]
        first = (slot // 2) * REPS + lax.rem(slot, 2)
        block = grads_ref[b]
        out_ref[first] = block
        out_ref[first + 2] = block
        return 0

    lax.fori_loop(0, grads_ref.shape[0], body, 0, unroll=8)


def deal(at, owner_slot, grads, root_left):
    blocks, row_part, part = grads.shape
    _, rows, size = root_left.shape
    count, half = rows // row_part, row_part // 2
    return pl.pallas_call(
        deal_kernel,
        out_shape=(
            shape((2 * blocks, row_part, part), BF16),
        )
        + (shape((count, half, size), BF16),) * REPS,
        in_specs=[SMEM, SMEM, VMEM, VMEM],
        out_specs=(VMEM,) * (1 + REPS),
        compiler_params=params(60 * 1024 * 1024),
        cost_estimate=cost(0, 6 * grads.size + 4 * root_left.size),
        name="deal_blocks",
    )(at, owner_slot, grads, root_left.reshape(2, count, 2, half, size))


def load(src, dst, sem):
    copy = pltpu.make_async_copy(src, dst, sem)
    copy.start()
    return copy


def load_columns(arrived, whole, sems):
    part = arrived.shape[3]
    return [
        load(arrived.at[:, j], whole.at[:, :, pl.ds(j * part, part)], sems.at[j]) for j in range(arrived.shape[1])
    ]


def gram_kernel(
    at_ref, arrived, stat_left, stat_right, left_out, right_out, left_term, right_term, whole, lhs, gl, gr, sems, out_sems
):
    rep, k, near = at_ref[0], at_ref[1], at_ref[2]
    _, row_part, size = whole.shape
    part = size // REPS
    rows = gl.shape[0]
    columns = load_columns(arrived, whole, sems)
    get_gr = load(stat_right.at[k], gr, sems.at[REPS])
    get_gl = load(stat_left.at[k], gl, sems.at[REPS + 1])
    for copy in columns:
        copy.wait()

    grad = whole[...].reshape(size, size)
    for i, index in enumerate((rep, near)):
        cols = whole[:, :, pl.ds(pl.multiple_of(index * part, part), part)].reshape(size, part)
        term = 0.05 * dot(cols, grad, TN)
        if i == 0:
            get_gr.wait()
            gr[...] = 0.95 * gr[...] + term
            put_right = load(gr, right_out.at[k], out_sems.at[0])
        else:
            right_term[...] = term.astype(BF16)
    for i, index in enumerate((rep, near)):
        from_row = pl.ds(index * (rows // row_part), rows // row_part)
        lhs[i * rows : (i + 1) * rows, :] = whole[from_row].reshape(rows, size)
    term = 0.05 * dot(lhs[...], grad, NT)
    get_gl.wait()
    gl[...] = 0.95 * gl[...] + term[:rows]
    put_left = load(gl, left_out.at[k], out_sems.at[1])
    left_term[...] = term[rows:].astype(BF16)
    put_left.wait()
    put_right.wait()


def grams(at, arrived, gram_left, gram_right):
    owners, reps, row_part, part = arrived.shape
    _, rows, size = gram_left.shape
    state = shape(gram_left.shape, F32)
    return pl.pallas_call(
        gram_kernel,
        in_specs=[SMEM] + [ANY] * 3,
        out_specs=(ANY,) * 2 + (VMEM,) * 2,
        scratch_shapes=[
            pltpu.VMEM((owners, row_part, size), BF16),
            pltpu.VMEM((2 * rows, size), BF16),
            pltpu.VMEM((rows, size), F32),
            pltpu.VMEM((rows, size), F32),
            pltpu.SemaphoreType.DMA((REPS + 2,)),
            pltpu.SemaphoreType.DMA((2,)),
        ],
        out_shape=(state,) * 2 + (shape((rows, size), BF16),) * 2,
        compiler_params=params(MID_LIMIT),
        cost_estimate=GRAM_COST,
        name="own_grams",
    )(at, arrived, gram_left, gram_right)


def mid_kernel(
    at_ref,
    arrived,
    l0_ref,
    l1_ref,
    l2_ref,
    l3_ref,
    right_ref,
    mom_ref,
    sec_ref,
    mom_out,
    sec_out,
    pieces,
    pre_sum,
    own_sum,
    whole,
    left,
    right,
    mixed,
    mom,
    sec,
    sems,
    out_sems,
):
    rep, k, step = at_ref[0], at_ref[1], at_ref[3]
    owners, row_part, size = whole.shape
    part = size // REPS
    rows = mom.shape[0]
    share = l0_ref.shape[0]
    columns = load_columns(arrived, whole, sems)
    get_mom = load(mom_ref.at[k], mom, sems.at[REPS])
    get_sec = load(sec_ref.at[k], sec, sems.at[REPS + 1])
    get_left = []
    for j, ref in enumerate((l0_ref, l1_ref, l2_ref, l3_ref)):
        first = lax.rem(rep - j * step + REPS * REPS, REPS) * share
        get_left.append(load(ref, left.at[pl.ds(first, share)], sems.at[REPS + 2 + j]))
    get_right = load(right_ref.at[k], right, sems.at[2 * REPS + 2])
    for copy in columns + get_left:
        copy.wait()
    grad = whole[...].reshape(size, size)
    mixed[...] = dot(left[...].reshape(mixed.shape), grad).astype(BF16)

    get_mom.wait()
    get_sec.wait()
    own = whole[pl.ds(rep * (rows // row_part), rows // row_part)].reshape(rows, size).astype(F32)
    first = 0.9 * mom[...] + 0.1 * own
    second = 0.95 * sec[...] + 0.05 * own * own
    mom[...] = first
    sec[...] = second
    put_mom = load(mom, mom_out.at[k], out_sems.at[0])
    put_sec = load(sec, sec_out.at[k], out_sems.at[1])
    way = first / (jnp.sqrt(second) + 1e-08)
    own_sum[...] = jnp.sum((way * way).reshape(rows // 8, 8, size), axis=0)

    get_right.wait()
    total = jnp.zeros((8, part), F32)
    for j in range(REPS):
        piece = dot(mixed[...], right[:, j * part : (j + 1) * part])
        total += jnp.sum((piece * piece).reshape(-1, 8, part), axis=0)
        halves = piece.reshape(owners, 2, 8, part)
        for i in range(2):
            pieces[:, j, :, i * part : (i + 1) * part] = halves[:, i].astype(BF16)
    pre_sum[...] = total
    put_mom.wait()
    put_sec.wait()


def mid(at, arrived, left_parts, root_right, moment, second):
    owners, reps, row_part, part = arrived.shape
    _, rows, size = moment.shape
    half = row_part // 2
    state = shape(moment.shape, F32)
    return pl.pallas_call(
        mid_kernel,
        in_specs=[SMEM] + [ANY] * 8,
        out_specs=(ANY,) * 2 + (VMEM,) * 3,
        scratch_shapes=[
            pltpu.VMEM((owners, row_part, size), BF16),
            pltpu.VMEM((owners, half, size), BF16),
            pltpu.VMEM((size, size), BF16),
            pltpu.VMEM((owners * half, size), BF16),
            pltpu.VMEM((rows, size), F32),
            pltpu.VMEM((rows, size), F32),
            pltpu.SemaphoreType.DMA((2 * REPS + 3,)),
            pltpu.SemaphoreType.DMA((2,)),
        ],
        out_shape=(state,) * 2
        + (
            shape((owners, reps, half // 2, 2 * part + LANES), BF16),
            shape((8, part), F32),
            shape((8, size), F32),
        ),
        compiler_params=params(MID_LIMIT),
        cost_estimate=MID_COST,
        name="own_slot",
    )(at, arrived, *left_parts, root_right, moment, second)


def late_kernel(
    at_ref, grad_ref, mom_ref, sec_ref, own_ref, pre_ref, _, __, ___, mom_out, sec_out, pieces, mom, sec, pads, sems, out_sems
):
    k = 1 - at_ref[1]
    count, reps, row_part, part = grad_ref.shape
    rows = count * row_part
    steps = mom.shape[0]
    chunk = count // steps
    size = reps * part

    def block(ref, n):
        return ref.at[k, pl.ds(n * chunk * row_part, chunk * row_part)]

    loads = []
    for n in range(steps):
        for i, (src, dst) in enumerate(((mom_ref, mom), (sec_ref, sec))):
            copy = pltpu.make_async_copy(block(src, n), dst.at[n], sems.at[2 * n + i])
            copy.start()
            loads.append(copy)
    stores = []
    total = jnp.zeros((8, part), F32)
    for n in range(steps):
        loads[2 * n].wait()
        loads[2 * n + 1].wait()
        for j in range(reps):
            cols = slice(j * part, (j + 1) * part)
            grad = grad_ref[n * chunk : (n + 1) * chunk, j].reshape(chunk * row_part, part).astype(F32)
            first = 0.9 * mom[n, :, cols] + 0.1 * grad
            second = 0.95 * sec[n, :, cols] + 0.05 * grad * grad
            mom[n, :, cols] = first
            sec[n, :, cols] = second
            way = first / (jnp.sqrt(second) + 1e-08)
            total += jnp.sum((way * way).reshape(-1, 8, part), axis=0)
        for i, (src, dst) in enumerate(((mom, mom_out), (sec, sec_out))):
            copy = pltpu.make_async_copy(src.at[n], block(dst, n), out_sems.at[2 * n + i])
            copy.start()
            stores.append(copy)
    own, other = jnp.sum(own_ref[...]), jnp.sum(total)
    even = at_ref[1] == 0
    values = (jnp.where(even, own, other), jnp.where(even, other, own), jnp.sum(pre_ref[...]))
    tile = pads.shape[2:]
    row = lax.broadcasted_iota(jnp.int32, tile, 0)
    pad = jnp.zeros(tile, F32)
    for i, value in enumerate(values):
        rest = jnp.full(tile, value, F32)
        for n in range(3):
            high = rest.astype(BF16).astype(F32)
            pad = jnp.where(row == 3 * i + n, high, pad)
            rest = rest - high
    pads[...] = jnp.broadcast_to(pad.astype(BF16), pads.shape)
    copy = pltpu.make_async_copy(pads, pieces.at[:, :, :, pl.ds(2 * part, LANES)], out_sems.at[2 * steps])
    copy.start()
    for store in stores + [copy]:
        store.wait()


def late(at, grad, moment, second, own_sq, pre_sq, moment_new, second_new, pieces, steps=4):
    _, rows, size = moment.shape
    state = shape(moment.shape, F32)
    return pl.pallas_call(
        late_kernel,
        in_specs=[SMEM, VMEM, ANY, ANY, VMEM, VMEM, ANY, ANY, ANY],
        out_specs=(ANY,) * 3,
        scratch_shapes=[
            pltpu.VMEM((steps, rows // steps, size), F32),
            pltpu.VMEM((steps, rows // steps, size), F32),
            pltpu.VMEM(pieces.shape[:3] + (LANES,), BF16),
            pltpu.SemaphoreType.DMA((2 * steps,)),
            pltpu.SemaphoreType.DMA((2 * steps + 1,)),
        ],
        out_shape=(state, state, shape(pieces.shape, BF16)),
        input_output_aliases={6: 0, 7: 1, 8: 2},
        compiler_params=params(LATE_LIMIT),
        cost_estimate=cost(15 * rows * size, 20 * rows * size),
        name="other_adam",
    )(at, grad, moment, second, own_sq, pre_sq, moment_new, second_new, pieces)


def add_kernel(at_ref, left_part, right_part, left_ref, right_ref, _, __, left_out, right_out):
    left_out[0] = 0.95 * left_ref[0] + left_part[...].astype(F32)
    right_out[0] = 0.95 * right_ref[0] + right_part[...].astype(F32)


def add(at, left_part, right_part, gram_left, gram_right, left_new, right_new, steps=4):
    _, rows, size = gram_left.shape
    state = pl.BlockSpec((1, rows // steps, size), lambda n, at: (1 - at[1], n, 0))
    term = pl.BlockSpec((rows // steps, size), lambda n, at: (n, 0))
    return pl.pallas_call(
        add_kernel,
        grid_spec=pltpu.PrefetchScalarGridSpec(
            num_scalar_prefetch=1,
            grid=(steps,),
            in_specs=[term, term, state, state, ANY, ANY],
            out_specs=(state, state),
        ),
        out_shape=(shape(gram_left.shape, F32), shape(gram_right.shape, F32)),
        input_output_aliases={5: 0, 6: 1},
        compiler_params=params(),
        cost_estimate=cost(4 * rows * size, 20 * rows * size),
        name="add_terms",
    )(at, left_part, right_part, gram_left, gram_right, left_new, right_new)


def finish_kernel(cells, slot_ref, in_ref, out_ref, ratios):
    rows = in_ref.shape[1]
    part = (in_ref.shape[2] - LANES) // 2
    sums = in_ref[:, :, 2 * part :].astype(F32).reshape(-1, REPS, rows, LANES)
    adam_sums = jnp.sum(sums, axis=1)
    for k in range(2):
        adam_all = jnp.sum(adam_sums[:, 3 * k : 3 * k + 3], axis=1, keepdims=True)
        pre_all = jnp.sum((sums[:, k] + sums[:, k + 2])[:, 6:8], axis=1, keepdims=True)
        value = jnp.sqrt(adam_all / cells + 1e-06) / jnp.sqrt(pre_all / cells + 1e-06)
        ratios[:, k] = jnp.broadcast_to(value, (value.shape[0], rows, LANES))

    def place_block(b, _):
        slot = slot_ref[b]
        owner, k = slot // 2, lax.rem(slot, 2)
        by = ratios[owner, k]
        by = jnp.concatenate([by] * (2 * part // LANES), axis=1)
        for n in range(2):
            piece = in_ref[owner * REPS + k + 2 * n, :, : 2 * part].astype(F32) * by
            piece = jnp.concatenate([piece[:, :part], piece[:, part:]], axis=0)
            out_ref[b, 2 * n * rows : 2 * (n + 1) * rows, :] = piece.astype(BF16)
        return 0

    lax.fori_loop(0, out_ref.shape[0], place_block, 0, unroll=8)


def finish(owner_slot, pieces, size):
    count, rows, wide = pieces.shape
    blocks = owner_slot.shape[0]
    part = (wide - LANES) // 2
    return pl.pallas_call(
        functools.partial(finish_kernel, float(size * size)),
        out_shape=shape((blocks, 4 * rows, part), BF16),
        in_specs=[SMEM, VMEM],
        out_specs=VMEM,
        scratch_shapes=[pltpu.VMEM((blocks // 2, 2, rows, LANES), F32)],
        compiler_params=params(),
        cost_estimate=cost(8 * blocks * rows * part, 20 * blocks * rows * part),
        name="finish_updates",
    )(owner_slot, pieces)


def per_device(grads, owner_slot, gram_left, gram_right, root_left, root_right, moment, second):
    blocks, row_part, part = grads.shape
    _, rows, size = root_left.shape
    at = place()
    sent, keep, ahead, across, back = deal(at, owner_slot, grads, root_left)
    arrived = everyone(sent).reshape(OWNERS, REPS, row_part, part)
    ahead = to_neighbour(ahead)
    across = to_neighbour(across, 2)
    back = to_neighbour(back, -1)

    count = rows // row_part
    other = to_neighbour(lax.dynamic_slice_in_dim(arrived, at[2] * count, count, 0))
    left_new, right_new, left_term, right_term = grams(at, arrived, gram_left, gram_right)
    arrived, left_term, right_term = lax.optimization_barrier((arrived, left_term, right_term))
    right_term = to_neighbour(right_term)
    left_term = to_neighbour(left_term)
    moment_new, second_new, pieces, pre_sq, own_sq = mid(
        at, arrived, (keep, ahead, across, back), root_right, moment, second
    )
    moment_new, second_new, pieces = late(
        at, other, moment, second, own_sq, pre_sq, moment_new, second_new, pieces
    )
    pieces, right_term = lax.optimization_barrier((pieces, right_term))
    homed = everyone(pieces.reshape((-1,) + pieces.shape[2:]))
    left_new, right_new = add(at, left_term, right_term, gram_left, gram_right, left_new, right_new)
    updates = finish(owner_slot, homed, size)
    return (updates, left_new, right_new, moment_new, second_new)


def solution(mesh):
    return jax.shard_map(
        per_device,
        mesh=mesh,
        in_specs=(
            P(None, "fsdp", "rep"),
            P(),
            P("fsdp", "rep", None),
            P("fsdp", "rep", None),
            P("fsdp", "rep", None),
            P("fsdp", None, None),
            P("fsdp", "rep", None),
            P("fsdp", "rep", None),
        ),
        out_specs=(
            P(None, "fsdp", "rep"),
            P("fsdp", "rep", None),
            P("fsdp", "rep", None),
            P("fsdp", "rep", None),
            P("fsdp", "rep", None),
        ),
        check_vma=False,
    )
```

```python
import functools

import jax
import jax.numpy as jnp
from jax import lax
from jax.experimental import pallas as pl
from jax.experimental.pallas import tpu as pltpu
from jax.sharding import PartitionSpec as P

VMEM_LIMIT = 32 * 1024 * 1024
MID_LIMIT = 60 * 1024 * 1024
BIG_LIMIT = 60 * 1024 * 1024
DEALS = 4
LATE_LIMIT = 60 * 1024 * 1024
REPS = 4
OWNERS = 32
LANES = 128
NN = (((1,), (0,)), ((), ()))
NT = (((1,), (1,)), ((), ()))
TN = (((0,), (0,)), ((), ()))
ANY = pl.BlockSpec(memory_space=pl.ANY)
VMEM = pl.BlockSpec(memory_space=pltpu.VMEM)
SMEM = pl.BlockSpec(memory_space=pltpu.SMEM)
BF16 = jnp.bfloat16
F32 = jnp.float32


def params(limit=VMEM_LIMIT):
    return pltpu.CompilerParams(vmem_limit_bytes=limit)


def cost(flops, nbytes):
    return pl.CostEstimate(flops=flops, bytes_accessed=nbytes, transcendentals=0)


def dot(a, b, dims=NN):
    return lax.dot_general(a, b, dims, preferred_element_type=F32)


def shape(dims, dtype):
    return jax.ShapeDtypeStruct(dims, dtype)


GRAM_COST = cost(1, 1)
MID_COST = cost(10**11, 10**6)


def place():
    rep = lax.axis_index("rep").astype(jnp.int32)
    core = lax.rem(lax.axis_index("fsdp").astype(jnp.int32), 2)
    step = 1 - 2 * core
    return jnp.stack([rep, lax.rem(rep, 2), lax.rem(rep + step + REPS, REPS), step])


def to_neighbour(x, far=1):
    pairs = []
    for owner in range(OWNERS):
        step = far * (1 - 2 * (owner % 2))
        for rep in range(REPS):
            pairs.append((owner * REPS + rep, owner * REPS + (rep + step) % REPS))
    return lax.ppermute(x, ("fsdp", "rep"), pairs)


def everyone(x):
    return lax.all_to_all(x, ("fsdp", "rep"), split_axis=0, concat_axis=0, tiled=True)


def load(src, dst, sem):
    copy = pltpu.make_async_copy(src, dst, sem)
    copy.start()
    return copy


def load_columns(arrived, whole, sems):
    part = arrived.shape[3]
    return [
        load(arrived.at[:, j], whole.at[:, :, pl.ds(j * part, part)], sems.at[j]) for j in range(arrived.shape[1])
    ]


def deal_kernel(slot_ref, grads_ref, out_ref, grads, out, block_of, sems):
    blocks = grads.shape[0]
    chunk = blocks // DEALS
    gets, puts = [], []
    for n in range(DEALS):
        part_of = pl.ds(n * chunk, chunk)
        gets.append(load(grads_ref.at[part_of], grads.at[part_of], sems.at[n]))

    def note(b, _):
        block_of[slot_ref[b]] = b
        return 0

    lax.fori_loop(0, blocks, note, 0, unroll=8)
    for copy in gets:
        copy.wait()

    def place_owner(owner, _):
        for k in range(2):
            block = grads[block_of[2 * owner + k]]
            out[owner * REPS + k] = block
            out[owner * REPS + k + 2] = block
        return 0

    step = blocks // 2 // DEALS
    for n in range(DEALS):
        lax.fori_loop(n * step, (n + 1) * step, place_owner, 0, unroll=4)
        part_of = pl.ds(n * step * REPS, step * REPS)
        puts.append(load(out.at[part_of], out_ref.at[part_of], sems.at[DEALS + n]))
    for copy in puts:
        copy.wait()


def deal(owner_slot, grads):
    blocks, row_part, part = grads.shape
    return pl.pallas_call(
        deal_kernel,
        out_shape=shape((2 * blocks, row_part, part), BF16),
        in_specs=[SMEM, ANY],
        out_specs=ANY,
        scratch_shapes=[
            pltpu.VMEM(grads.shape, BF16),
            pltpu.VMEM((2 * blocks, row_part, part), BF16),
            pltpu.SMEM((blocks,), jnp.int32),
            pltpu.SemaphoreType.DMA((2 * DEALS,)),
        ],
        compiler_params=params(BIG_LIMIT),
        cost_estimate=cost(0, 6 * grads.size),
        name="deal_blocks",
    )(owner_slot, grads)


def share_kernel(at_ref, left_ref, keep_ref, ahead_ref, across_ref, back_ref, left, sems):
    get = load(left_ref, left, sems.at[0])
    get.wait()
    puts = []
    for j, ref in ((1, ahead_ref), (2, across_ref), (-1, back_ref), (0, keep_ref)):
        to = lax.rem(at_ref[0] + j * at_ref[3] + REPS, REPS)
        puts.append(load(left.at[lax.rem(to, 2), :, to // 2], ref, sems.at[1 + len(puts)]))
    for copy in puts:
        copy.wait()


def share_rows(at, root_left, row_part):
    _, rows, size = root_left.shape
    count, half = rows // row_part, row_part // 2
    return pl.pallas_call(
        share_kernel,
        out_shape=(shape((count, half, size), BF16),) * REPS,
        in_specs=[SMEM, ANY],
        out_specs=(ANY,) * REPS,
        scratch_shapes=[pltpu.VMEM((2, count, 2, half, size), BF16), pltpu.SemaphoreType.DMA((1 + REPS,))],
        compiler_params=params(BIG_LIMIT),
        cost_estimate=cost(0, 4 * root_left.size),
        name="share_rows",
    )(at, root_left.reshape(2, count, 2, half, size))


def gram_kernel(
    at_ref, arrived, stat_left, stat_right, left_out, right_out, left_term, right_term,
    whole, lhs, gl, gr, lt, rt, sems, out_sems,
):
    rep, k, near = at_ref[0], at_ref[1], at_ref[2]
    _, row_part, size = whole.shape
    part = size // REPS
    rows = gl.shape[0]
    columns = load_columns(arrived, whole, sems)
    get_gr = load(stat_right.at[k], gr, sems.at[REPS])
    get_gl = load(stat_left.at[k], gl, sems.at[REPS + 1])
    for copy in columns:
        copy.wait()
    puts = []

    def emit(j, term, stat, terms, new_ref, term_ref):
        cols = pl.ds(j * part, part)
        stat[:, cols] = 0.95 * stat[:, cols] + term[:rows]
        terms[:, cols] = term[rows:].astype(BF16)
        for src, dst in ((stat, new_ref.at[k]), (terms, term_ref)):
            puts.append(load(src.at[:, cols], dst.at[:, cols], out_sems.at[len(puts)]))

    for i, index in enumerate((rep, near)):
        cols = whole[:, :, pl.ds(pl.multiple_of(index * part, part), part)].reshape(size, part)
        lhs[i * rows : (i + 1) * rows, :] = cols.T
    get_gr.wait()
    for j in range(REPS):
        grad = whole[:, :, j * part : (j + 1) * part].reshape(size, part)
        emit(j, 0.05 * dot(lhs[...], grad), gr, rt, right_out, right_term)
    for i, index in enumerate((rep, near)):
        from_row = pl.ds(index * (rows // row_part), rows // row_part)
        lhs[i * rows : (i + 1) * rows, :] = whole[from_row].reshape(rows, size)
    get_gl.wait()
    blocks = part // row_part
    for j in range(REPS):
        grad = whole[j * blocks : (j + 1) * blocks].reshape(part, size)
        emit(j, 0.05 * dot(lhs[...], grad, NT), gl, lt, left_out, left_term)
    for copy in puts:
        copy.wait()


def grams(at, arrived, gram_left, gram_right):
    owners, reps, row_part, part = arrived.shape
    _, rows, size = gram_left.shape
    state = shape(gram_left.shape, F32)
    return pl.pallas_call(
        gram_kernel,
        in_specs=[SMEM] + [ANY] * 3,
        out_specs=(ANY,) * 4,
        scratch_shapes=[
            pltpu.VMEM((owners, row_part, size), BF16),
            pltpu.VMEM((2 * rows, size), BF16),
            pltpu.VMEM((rows, size), F32),
            pltpu.VMEM((rows, size), F32),
            pltpu.VMEM((rows, size), BF16),
            pltpu.VMEM((rows, size), BF16),
            pltpu.SemaphoreType.DMA((REPS + 2,)),
            pltpu.SemaphoreType.DMA((4 * REPS,)),
        ],
        out_shape=(state,) * 2 + (shape((rows, size), BF16),) * 2,
        compiler_params=params(MID_LIMIT),
        cost_estimate=GRAM_COST,
        name="own_grams",
    )(at, arrived, gram_left, gram_right)


def mid_kernel(
    at_ref, arrived, l0_ref, l1_ref, l2_ref, l3_ref, right_ref, mom_ref, sec_ref, mom_out, sec_out, pieces, sum_ref,
    whole, left, right, mixed, mom, sec, out, sems, out_sems,
):
    rep, k, step = at_ref[0], at_ref[1], at_ref[3]
    owners, row_part, size = whole.shape
    part = size // REPS
    rows = mom.shape[0]
    share = l0_ref.shape[0]
    get_left = []
    for j, ref in enumerate((l0_ref, l1_ref, l2_ref, l3_ref)):
        first = lax.rem(rep - j * step + REPS * REPS, REPS) * share
        get_left.append(load(ref, left.at[pl.ds(first, share)], sems.at[REPS + 2 + j]))
    columns = load_columns(arrived, whole, sems)
    get_mom = load(mom_ref.at[k], mom, sems.at[REPS])
    get_sec = load(sec_ref.at[k], sec, sems.at[REPS + 1])
    half = size // 2
    get_right = [
        load(right_ref.at[k, :, pl.ds(i * half, half)], right.at[:, pl.ds(i * half, half)], sems.at[2 * REPS + 2 + i])
        for i in range(2)
    ]
    for copy in get_left + columns:
        copy.wait()
    for j in range(REPS):
        grad = whole[:, :, j * part : (j + 1) * part].reshape(size, part)
        mixed[:, j * part : (j + 1) * part] = dot(left[...].reshape(mixed.shape), grad).astype(BF16)

    get_mom.wait()
    get_sec.wait()
    own_total = jnp.zeros((8, part), F32)
    puts = []
    for j in range(REPS):
        cols = pl.ds(j * part, part)
        own = whole[pl.ds(rep * (rows // row_part), rows // row_part), :, cols].reshape(rows, part).astype(F32)
        first = 0.9 * mom[:, cols] + 0.1 * own
        second = 0.95 * sec[:, cols] + 0.05 * own * own
        mom[:, cols] = first
        sec[:, cols] = second
        way = first / (jnp.sqrt(second) + 1e-08)
        own_total += jnp.sum((way * way).reshape(rows // 8, 8, part), axis=0)
        for src, dst in ((mom, mom_out), (sec, sec_out)):
            puts.append(load(src.at[:, cols], dst.at[k, :, cols], out_sems.at[len(puts)]))
    sum_ref[0] = own_total

    for copy in get_right:
        copy.wait()
    total = jnp.zeros((8, part), F32)
    for j in range(REPS):
        piece = dot(mixed[...], right[:, j * part : (j + 1) * part])
        total += jnp.sum((piece * piece).reshape(-1, 8, part), axis=0)
        halves = piece.reshape(owners, 2, 8, part)
        for i in range(2):
            out[:, j, :, i * part : (i + 1) * part] = halves[:, i].astype(BF16)
        puts.append(load(out.at[:, j], pieces.at[:, j, :, pl.ds(0, 2 * part)], out_sems.at[len(puts)]))
    sum_ref[1] = total
    for copy in puts:
        copy.wait()


def mid(at, arrived, left_parts, root_right, moment, second):
    owners, reps, row_part, part = arrived.shape
    _, rows, size = moment.shape
    half = row_part // 2
    state = shape(moment.shape, F32)
    return pl.pallas_call(
        mid_kernel,
        in_specs=[SMEM] + [ANY] * 8,
        out_specs=(ANY,) * 3 + (VMEM,),
        scratch_shapes=[
            pltpu.VMEM((owners, row_part, size), BF16),
            pltpu.VMEM((owners, half, size), BF16),
            pltpu.VMEM((size, size), BF16),
            pltpu.VMEM((owners * half, size), BF16),
            pltpu.VMEM((rows, size), F32),
            pltpu.VMEM((rows, size), F32),
            pltpu.VMEM((owners, reps, half // 2, 2 * part), BF16),
            pltpu.SemaphoreType.DMA((2 * REPS + 4,)),
            pltpu.SemaphoreType.DMA((3 * REPS,)),
        ],
        out_shape=(state,) * 2
        + (shape((owners, reps, half // 2, 2 * part + LANES), BF16), shape((2, 8, part), F32)),
        compiler_params=params(MID_LIMIT),
        cost_estimate=MID_COST,
        name="own_slot",
    )(at, arrived, *left_parts, root_right, moment, second)


def late_kernel(
    at_ref, grad_hbm, mom_ref, sec_ref, sum_ref, _, __, ___, mom_out, sec_out, pieces, grad_ref, mom, sec, pads, sems, out_sems
):
    k = 1 - at_ref[1]
    count, reps, row_part, part = grad_ref.shape
    rows = count * row_part
    steps = mom.shape[0]
    chunk = count // steps
    size = reps * part

    def block(ref, n):
        return ref.at[k, pl.ds(n * chunk * row_part, chunk * row_part)]

    get_grad = load(grad_hbm, grad_ref, sems.at[2 * steps])
    loads = []
    for n in range(steps):
        for i, (src, dst) in enumerate(((mom_ref, mom), (sec_ref, sec))):
            copy = pltpu.make_async_copy(block(src, n), dst.at[n], sems.at[2 * n + i])
            copy.start()
            loads.append(copy)
    stores = []
    total = jnp.zeros((8, part), F32)
    get_grad.wait()
    for n in range(steps):
        loads[2 * n].wait()
        loads[2 * n + 1].wait()
        for j in range(reps):
            cols = slice(j * part, (j + 1) * part)
            grad = grad_ref[n * chunk : (n + 1) * chunk, j].reshape(chunk * row_part, part).astype(F32)
            first = 0.9 * mom[n, :, cols] + 0.1 * grad
            second = 0.95 * sec[n, :, cols] + 0.05 * grad * grad
            mom[n, :, cols] = first
            sec[n, :, cols] = second
            way = first / (jnp.sqrt(second) + 1e-08)
            total += jnp.sum((way * way).reshape(-1, 8, part), axis=0)
        for i, (src, dst) in enumerate(((mom, mom_out), (sec, sec_out))):
            copy = pltpu.make_async_copy(src.at[n], block(dst, n), out_sems.at[2 * n + i])
            copy.start()
            stores.append(copy)
    own, other = jnp.sum(sum_ref[0]), jnp.sum(total)
    even = at_ref[1] == 0
    values = (jnp.where(even, own, other), jnp.where(even, other, own), jnp.sum(sum_ref[1]))
    tile = pads.shape[2:]
    row = lax.broadcasted_iota(jnp.int32, tile, 0)
    pad = jnp.zeros(tile, F32)
    for i, value in enumerate(values):
        rest = jnp.full(tile, value, F32)
        for n in range(3):
            high = rest.astype(BF16).astype(F32)
            pad = jnp.where(row == 3 * i + n, high, pad)
            rest = rest - high
    pads[...] = jnp.broadcast_to(pad.astype(BF16), pads.shape)
    copy = pltpu.make_async_copy(pads, pieces.at[:, :, :, pl.ds(2 * part, LANES)], out_sems.at[2 * steps])
    copy.start()
    for store in stores + [copy]:
        store.wait()


def late(at, grad, moment, second, sums, moment_new, second_new, pieces, steps=4):
    _, rows, size = moment.shape
    state = shape(moment.shape, F32)
    return pl.pallas_call(
        late_kernel,
        in_specs=[SMEM, ANY, ANY, ANY, VMEM, ANY, ANY, ANY],
        out_specs=(ANY,) * 3,
        scratch_shapes=[
            pltpu.VMEM(grad.shape, BF16),
            pltpu.VMEM((steps, rows // steps, size), F32),
            pltpu.VMEM((steps, rows // steps, size), F32),
            pltpu.VMEM(pieces.shape[:3] + (LANES,), BF16),
            pltpu.SemaphoreType.DMA((2 * steps + 1,)),
            pltpu.SemaphoreType.DMA((2 * steps + 1,)),
        ],
        out_shape=(state, state, shape(pieces.shape, BF16)),
        input_output_aliases={5: 0, 6: 1, 7: 2},
        compiler_params=params(LATE_LIMIT),
        cost_estimate=cost(15 * rows * size, 20 * rows * size),
        name="other_adam",
    )(at, grad, moment, second, sums, moment_new, second_new, pieces)


def add_kernel(at_ref, term_ref, stat_ref, _, new_ref, term, stat, sems, out_sems):
    k = 1 - at_ref[1]
    steps = stat.shape[0]
    rows = stat.shape[1]
    gets = [
        (load(stat_ref.at[k, pl.ds(n * rows, rows)], stat.at[n], sems.at[n]), load(term_ref.at[pl.ds(n * rows, rows)], term.at[n], sems.at[steps + n]))
        for n in range(steps)
    ]
    puts = []
    for n in range(steps):
        for copy in gets[n]:
            copy.wait()
        stat[n] = 0.95 * stat[n] + term[n].astype(F32)
        puts.append(load(stat.at[n], new_ref.at[k, pl.ds(n * rows, rows)], out_sems.at[n]))
    for copy in puts:
        copy.wait()


def add(at, term, stat, new, estimate, steps=4):
    _, rows, size = stat.shape
    return pl.pallas_call(
        add_kernel,
        in_specs=[SMEM, ANY, ANY, ANY],
        out_specs=ANY,
        out_shape=shape(stat.shape, F32),
        scratch_shapes=[
            pltpu.VMEM((steps, rows // steps, size), BF16),
            pltpu.VMEM((steps, rows // steps, size), F32),
            pltpu.SemaphoreType.DMA((2 * steps,)),
            pltpu.SemaphoreType.DMA((steps,)),
        ],
        input_output_aliases={3: 0},
        compiler_params=params(BIG_LIMIT),
        cost_estimate=estimate,
        name="add_term",
    )(at, term, stat, new)


def finish_kernel(cells, slot_ref, in_ref, out_hbm, ratios, out_ref, sems):
    rows = in_ref.shape[1]
    part = (in_ref.shape[2] - LANES) // 2
    sums = in_ref[:, :, 2 * part :].astype(F32).reshape(-1, REPS, rows, LANES)
    adam_sums = jnp.sum(sums, axis=1)
    for k in range(2):
        adam_all = jnp.sum(adam_sums[:, 3 * k : 3 * k + 3], axis=1, keepdims=True)
        pre_all = jnp.sum((sums[:, k] + sums[:, k + 2])[:, 6:8], axis=1, keepdims=True)
        value = jnp.sqrt(adam_all / cells + 1e-06) / jnp.sqrt(pre_all / cells + 1e-06)
        ratios[:, k] = jnp.broadcast_to(value, (value.shape[0], rows, LANES))

    def place_block(b, _):
        slot = slot_ref[b]
        owner, k = slot // 2, lax.rem(slot, 2)
        by = ratios[owner, k]
        by = jnp.concatenate([by] * (2 * part // LANES), axis=1)
        for n in range(2):
            piece = in_ref[owner * REPS + k + 2 * n, :, : 2 * part].astype(F32) * by
            piece = jnp.concatenate([piece[:, :part], piece[:, part:]], axis=0)
            out_ref[b, 2 * n * rows : 2 * (n + 1) * rows, :] = piece.astype(BF16)
        return 0

    chunk = out_ref.shape[0] // DEALS
    puts = []
    for n in range(DEALS):
        lax.fori_loop(n * chunk, (n + 1) * chunk, place_block, 0, unroll=8)
        part_of = pl.ds(n * chunk, chunk)
        puts.append(load(out_ref.at[part_of], out_hbm.at[part_of], sems.at[n]))
    for copy in puts:
        copy.wait()


def finish(owner_slot, pieces, size):
    count, rows, wide = pieces.shape
    blocks = owner_slot.shape[0]
    part = (wide - LANES) // 2
    return pl.pallas_call(
        functools.partial(finish_kernel, float(size * size)),
        out_shape=shape((blocks, 4 * rows, part), BF16),
        in_specs=[SMEM, VMEM],
        out_specs=ANY,
        scratch_shapes=[
            pltpu.VMEM((blocks // 2, 2, rows, LANES), F32),
            pltpu.VMEM((blocks, 4 * rows, part), BF16),
            pltpu.SemaphoreType.DMA((DEALS,)),
        ],
        compiler_params=params(),
        cost_estimate=cost(8 * blocks * rows * part, 20 * blocks * rows * part),
        name="finish_updates",
    )(owner_slot, pieces)


def per_device(grads, owner_slot, gram_left, gram_right, root_left, root_right, moment, second):
    blocks, row_part, part = grads.shape
    _, rows, size = root_left.shape
    at = place()
    sent = deal(owner_slot, grads)
    keep, ahead, across, back = share_rows(at, root_left, row_part)
    arrived = everyone(sent).reshape(OWNERS, REPS, row_part, part)
    ahead = to_neighbour(ahead)
    across = to_neighbour(across, 2)
    back = to_neighbour(back, -1)

    count = rows // row_part
    other = to_neighbour(lax.dynamic_slice_in_dim(arrived, at[2] * count, count, 0))
    left_new, right_new, left_term, right_term = grams(at, arrived, gram_left, gram_right)
    arrived, left_term, right_term = lax.optimization_barrier((arrived, left_term, right_term))
    right_term = to_neighbour(right_term)
    left_term = to_neighbour(left_term)
    moment_new, second_new, pieces, sums = mid(
        at, arrived, (keep, ahead, across, back), root_right, moment, second
    )
    moment_new, second_new, pieces = late(
        at, other, moment, second, sums, moment_new, second_new, pieces
    )
    pieces, right_term = lax.optimization_barrier((pieces, right_term))
    homed = everyone(pieces.reshape((-1,) + pieces.shape[2:]))
    right_new = add(at, right_term, gram_right, right_new, MID_COST)
    right_new, left_new = lax.optimization_barrier((right_new, left_new))
    left_new = add(at, left_term, gram_left, left_new, GRAM_COST)
    updates = finish(owner_slot, homed, size)
    return (updates, left_new, right_new, moment_new, second_new)


def solution(mesh):
    return jax.shard_map(
        per_device,
        mesh=mesh,
        in_specs=(
            P(None, "fsdp", "rep"),
            P(),
            P("fsdp", "rep", None),
            P("fsdp", "rep", None),
            P("fsdp", "rep", None),
            P("fsdp", None, None),
            P("fsdp", "rep", None),
            P("fsdp", "rep", None),
        ),
        out_specs=(
            P(None, "fsdp", "rep"),
            P("fsdp", "rep", None),
            P("fsdp", "rep", None),
            P("fsdp", "rep", None),
            P("fsdp", "rep", None),
        ),
        check_vma=False,
    )
```

```python
import functools

import jax
import jax.numpy as jnp
from jax import lax
from jax.experimental import pallas as pl
from jax.experimental.pallas import tpu as pltpu
from jax.sharding import PartitionSpec as P

VMEM_LIMIT = 32 * 1024 * 1024
GRAM_LIMIT = 50 * 1024 * 1024
MID_LIMIT = 46 * 1024 * 1024
BIG_LIMIT = 60 * 1024 * 1024
DEALS = 4
LATE_LIMIT = 46 * 1024 * 1024
REPS = 4
OWNERS = 32
LANES = 128
NN = (((1,), (0,)), ((), ()))
NT = (((1,), (1,)), ((), ()))
TN = (((0,), (0,)), ((), ()))
ANY = pl.BlockSpec(memory_space=pl.ANY)
VMEM = pl.BlockSpec(memory_space=pltpu.VMEM)
SMEM = pl.BlockSpec(memory_space=pltpu.SMEM)
BF16 = jnp.bfloat16
F32 = jnp.float32


def params(limit=VMEM_LIMIT):
    return pltpu.CompilerParams(vmem_limit_bytes=limit)


def cost(flops, nbytes):
    return pl.CostEstimate(flops=flops, bytes_accessed=nbytes, transcendentals=0)


def dot(a, b, dims=NN):
    return lax.dot_general(a, b, dims, preferred_element_type=F32)


def shape(dims, dtype):
    return jax.ShapeDtypeStruct(dims, dtype)


GRAM_COST = cost(1, 1)
MID_COST = cost(10**11, 10**6)


def place():
    rep = lax.axis_index("rep").astype(jnp.int32)
    core = lax.rem(lax.axis_index("fsdp").astype(jnp.int32), 2)
    step = 1 - 2 * core
    return jnp.stack([rep, lax.rem(rep, 2), lax.rem(rep + step + REPS, REPS), step])


def to_neighbour(x, far=1):
    pairs = []
    for owner in range(OWNERS):
        step = far * (1 - 2 * (owner % 2))
        for rep in range(REPS):
            pairs.append((owner * REPS + rep, owner * REPS + (rep + step) % REPS))
    return lax.ppermute(x, ("fsdp", "rep"), pairs)


def everyone(x):
    return lax.all_to_all(x, ("fsdp", "rep"), split_axis=0, concat_axis=0, tiled=True)


def load(src, dst, sem):
    copy = pltpu.make_async_copy(src, dst, sem)
    copy.start()
    return copy


def deal_kernel(slot_ref, grads_ref, out_ref, grads, out, block_of, sems):
    blocks = grads.shape[0]
    chunk = blocks // DEALS
    gets, puts = [], []
    for n in range(DEALS):
        part_of = pl.ds(n * chunk, chunk)
        gets.append(load(grads_ref.at[part_of], grads.at[part_of], sems.at[n]))

    def note(b, _):
        block_of[slot_ref[b]] = b
        return 0

    lax.fori_loop(0, blocks, note, 0, unroll=8)
    for copy in gets:
        copy.wait()

    def place_owner(owner, _):
        for k in range(2):
            block = grads[block_of[2 * owner + k]]
            out[owner * REPS + k] = block
            out[owner * REPS + k + 2] = block
        return 0

    step = blocks // 2 // DEALS
    for n in range(DEALS):
        lax.fori_loop(n * step, (n + 1) * step, place_owner, 0, unroll=4)
        part_of = pl.ds(n * step * REPS, step * REPS)
        puts.append(load(out.at[part_of], out_ref.at[part_of], sems.at[DEALS + n]))
    for copy in puts:
        copy.wait()


def deal(owner_slot, grads):
    blocks, row_part, part = grads.shape
    return pl.pallas_call(
        deal_kernel,
        out_shape=shape((2 * blocks, row_part, part), BF16),
        in_specs=[SMEM, ANY],
        out_specs=ANY,
        scratch_shapes=[
            pltpu.VMEM(grads.shape, BF16),
            pltpu.VMEM((2 * blocks, row_part, part), BF16),
            pltpu.SMEM((blocks,), jnp.int32),
            pltpu.SemaphoreType.DMA((2 * DEALS,)),
        ],
        compiler_params=params(BIG_LIMIT),
        cost_estimate=cost(0, 6 * grads.size),
        name="deal_blocks",
    )(owner_slot, grads)


def share_kernel(at_ref, left_ref, keep_ref, ahead_ref, across_ref, back_ref, left, sems):
    get = load(left_ref, left, sems.at[0])
    get.wait()
    puts = []
    for j, ref in ((1, ahead_ref), (2, across_ref), (-1, back_ref), (0, keep_ref)):
        to = lax.rem(at_ref[0] + j * at_ref[3] + REPS, REPS)
        puts.append(load(left.at[lax.rem(to, 2), :, to // 2], ref, sems.at[1 + len(puts)]))
    for copy in puts:
        copy.wait()


def share_rows(at, root_left, row_part):
    _, rows, size = root_left.shape
    count, half = rows // row_part, row_part // 2
    return pl.pallas_call(
        share_kernel,
        out_shape=(shape((count, half, size), BF16),) * REPS,
        in_specs=[SMEM, ANY],
        out_specs=(ANY,) * REPS,
        scratch_shapes=[pltpu.VMEM((2, count, 2, half, size), BF16), pltpu.SemaphoreType.DMA((1 + REPS,))],
        compiler_params=params(BIG_LIMIT),
        cost_estimate=cost(0, 4 * root_left.size),
        name="share_rows",
    )(at, root_left.reshape(2, count, 2, half, size))


def near_kernel(
    at_ref, g_ref, mom_ref, sec_ref, terms_ref, mom_out, sec_out, sum_ref,
    whole, lhs, terms, mom, sec, sems, out_sems,
):
    rep, k, near = at_ref[0], at_ref[1], at_ref[2]
    owners, reps, row_part, part = g_ref.shape
    size = owners * row_part
    rows = mom.shape[0]
    blocks = rows // row_part
    get_mom = load(mom_ref.at[k], mom, sems.at[0])
    get_sec = load(sec_ref.at[k], sec, sems.at[1])
    puts = []

    def put(src, dst):
        puts.append(load(src, dst, out_sems.at[len(puts)]))

    lhs[...] = g_ref[:, pl.ds(near, 1)].reshape(size, part).T
    for j in range(reps):
        cols = pl.ds(j * part, part)
        terms[0, :, cols] = (0.05 * dot(lhs[...], g_ref[:, j].reshape(size, part))).astype(BF16)
        put(terms.at[0, :, cols], terms_ref.at[0, :, cols])
    for j in range(reps):
        cols = slice(j * part, (j + 1) * part)
        whole[:, cols] = g_ref[:, j].reshape(size, part)
    rows_near = whole[pl.ds(pl.multiple_of(near * rows, rows), rows), :]
    for j in range(reps):
        cols = pl.ds(j * part, part)
        terms[1, :, cols] = (0.05 * dot(rows_near, whole[j * part : (j + 1) * part, :], NT)).astype(BF16)
        put(terms.at[1, :, cols], terms_ref.at[1, :, cols])
    get_mom.wait()
    get_sec.wait()
    total = jnp.zeros((8, part), F32)
    for j in range(reps):
        cols = pl.ds(j * part, part)
        own = g_ref[pl.ds(rep * blocks, blocks), j].reshape(rows, part).astype(F32)
        first = 0.9 * mom[:, cols] + 0.1 * own
        second = 0.95 * sec[:, cols] + 0.05 * own * own
        mom[:, cols] = first
        sec[:, cols] = second
        way = first / (jnp.sqrt(second) + 1e-08)
        total += jnp.sum((way * way).reshape(rows // 8, 8, part), axis=0)
        put(mom.at[:, cols], mom_out.at[k, :, cols])
        put(sec.at[:, cols], sec_out.at[k, :, cols])
    sum_ref[...] = total
    for copy in puts:
        copy.wait()


def near_terms(at, arrived, moment, second):
    _, reps, _, part = arrived.shape
    _, rows, size = moment.shape
    state = shape(moment.shape, F32)
    return pl.pallas_call(
        near_kernel,
        in_specs=[SMEM, VMEM, ANY, ANY],
        out_specs=(ANY,) * 3 + (VMEM,),
        scratch_shapes=[
            pltpu.VMEM((size, size), BF16),
            pltpu.VMEM((rows, size), BF16),
            pltpu.VMEM((2, rows, size), BF16),
            pltpu.VMEM((rows, size), F32),
            pltpu.VMEM((rows, size), F32),
            pltpu.SemaphoreType.DMA((2,)),
            pltpu.SemaphoreType.DMA((4 * reps,)),
        ],
        out_shape=(shape((2, rows, size), BF16), state, state, shape((8, part), F32)),
        compiler_params=params(GRAM_LIMIT),
        cost_estimate=GRAM_COST,
        name="near_terms",
    )(at, arrived, moment, second)


def precond_kernel(
    at_ref, g_ref, l0_ref, l1_ref, l2_ref, l3_ref, right_ref, pieces, sum_ref, left, right, mixed, out, sems, out_sems
):
    rep, k, step = at_ref[0], at_ref[1], at_ref[3]
    owners, reps, row_part, part = g_ref.shape
    size = owners * row_part
    share = l0_ref.shape[0]
    get_left = []
    for j, ref in enumerate((l0_ref, l1_ref, l2_ref, l3_ref)):
        first = lax.rem(rep - j * step + REPS * REPS, REPS) * share
        get_left.append(load(ref, left.at[pl.ds(first, share)], sems.at[j]))
    half = size // 2
    get_right = [
        load(right_ref.at[k, :, pl.ds(i * half, half)], right.at[:, pl.ds(i * half, half)], sems.at[REPS + i])
        for i in range(2)
    ]
    for copy in get_left:
        copy.wait()
    for j in range(reps):
        grad = g_ref[:, j].reshape(size, part)
        mixed[:, j * part : (j + 1) * part] = dot(left[...].reshape(mixed.shape), grad).astype(BF16)
    for copy in get_right:
        copy.wait()
    total = jnp.zeros((8, part), F32)
    puts = []
    for j in range(reps):
        piece = dot(mixed[...], right[:, j * part : (j + 1) * part])
        total += jnp.sum((piece * piece).reshape(-1, 8, part), axis=0)
        halves = piece.reshape(owners, 2, 8, part)
        for i in range(2):
            out[:, j, :, i * part : (i + 1) * part] = halves[:, i].astype(BF16)
        puts.append(load(out.at[:, j], pieces.at[:, j, :, pl.ds(0, 2 * part)], out_sems.at[j]))
    sum_ref[...] = total
    for copy in puts:
        copy.wait()


def precond(at, arrived, left_parts, root_right):
    owners, reps, row_part, part = arrived.shape
    size = root_right.shape[1]
    half = row_part // 2
    return pl.pallas_call(
        precond_kernel,
        in_specs=[SMEM, VMEM] + [ANY] * 5,
        out_specs=(ANY, VMEM),
        scratch_shapes=[
            pltpu.VMEM((owners, half, size), BF16),
            pltpu.VMEM((size, size), BF16),
            pltpu.VMEM((owners * half, size), BF16),
            pltpu.VMEM((owners, reps, half // 2, 2 * part), BF16),
            pltpu.SemaphoreType.DMA((REPS + 2,)),
            pltpu.SemaphoreType.DMA((reps,)),
        ],
        out_shape=(shape((owners, reps, half // 2, 2 * part + LANES), BF16), shape((8, part), F32)),
        compiler_params=params(MID_LIMIT),
        cost_estimate=MID_COST,
        name="precond_rows",
    )(at, arrived, *left_parts, root_right)


def gram_kernel(at_ref, arrived, stat_left, stat_right, left_out, right_out, whole, gl, gr, sems, out_sems):
    rep, k = at_ref[0], at_ref[1]
    _, row_part, size = whole.shape
    part = size // REPS
    rows = gl.shape[0]
    blocks = rows // row_part
    columns = [load(arrived.at[:, j], whole.at[:, :, pl.ds(j * part, part)], sems.at[j]) for j in range(REPS)]
    get_gr = load(stat_right.at[k], gr, sems.at[REPS])
    get_gl = load(stat_left.at[k], gl, sems.at[REPS + 1])
    for copy in columns:
        copy.wait()
    grad = whole[...].reshape(size, size)
    own = whole[:, :, pl.ds(pl.multiple_of(rep * part, part), part)].reshape(size, part)
    term = 0.05 * dot(own, grad, TN)
    get_gr.wait()
    gr[...] = 0.95 * gr[...] + term
    put_right = load(gr, right_out.at[k], out_sems.at[0])
    own = whole[pl.ds(rep * blocks, blocks)].reshape(rows, size)
    term = 0.05 * dot(own, grad, NT)
    get_gl.wait()
    gl[...] = 0.95 * gl[...] + term
    put_left = load(gl, left_out.at[k], out_sems.at[1])
    put_right.wait()
    put_left.wait()


def grams(at, arrived, gram_left, gram_right):
    owners, _, row_part, _ = arrived.shape
    _, rows, size = gram_left.shape
    state = shape(gram_left.shape, F32)
    return pl.pallas_call(
        gram_kernel,
        in_specs=[SMEM] + [ANY] * 3,
        out_specs=(ANY,) * 2,
        scratch_shapes=[
            pltpu.VMEM((owners, row_part, size), BF16),
            pltpu.VMEM((rows, size), F32),
            pltpu.VMEM((rows, size), F32),
            pltpu.SemaphoreType.DMA((REPS + 2,)),
            pltpu.SemaphoreType.DMA((2,)),
        ],
        out_shape=(state,) * 2,
        compiler_params=params(BIG_LIMIT),
        cost_estimate=MID_COST,
        name="own_grams",
    )(at, arrived, gram_left, gram_right)


def late_kernel(
    at_ref, grad_hbm, mom_ref, sec_ref, own_ref, pre_ref, _, __, ___, mom_out, sec_out, pieces, grad_ref, mom, sec, pads, sems, out_sems
):
    k = 1 - at_ref[1]
    count, reps, row_part, part = grad_ref.shape
    rows = count * row_part
    steps = mom.shape[0]
    chunk = count // steps
    size = reps * part

    def block(ref, n):
        return ref.at[k, pl.ds(n * chunk * row_part, chunk * row_part)]

    get_grad = load(grad_hbm, grad_ref, sems.at[2 * steps])
    loads = []
    for n in range(steps):
        for i, (src, dst) in enumerate(((mom_ref, mom), (sec_ref, sec))):
            copy = pltpu.make_async_copy(block(src, n), dst.at[n], sems.at[2 * n + i])
            copy.start()
            loads.append(copy)
    stores = []
    total = jnp.zeros((8, part), F32)
    get_grad.wait()
    for n in range(steps):
        loads[2 * n].wait()
        loads[2 * n + 1].wait()
        for j in range(reps):
            cols = slice(j * part, (j + 1) * part)
            grad = grad_ref[n * chunk : (n + 1) * chunk, j].reshape(chunk * row_part, part).astype(F32)
            first = 0.9 * mom[n, :, cols] + 0.1 * grad
            second = 0.95 * sec[n, :, cols] + 0.05 * grad * grad
            mom[n, :, cols] = first
            sec[n, :, cols] = second
            way = first / (jnp.sqrt(second) + 1e-08)
            total += jnp.sum((way * way).reshape(-1, 8, part), axis=0)
        for i, (src, dst) in enumerate(((mom, mom_out), (sec, sec_out))):
            copy = pltpu.make_async_copy(src.at[n], block(dst, n), out_sems.at[2 * n + i])
            copy.start()
            stores.append(copy)
    own, other = jnp.sum(own_ref[...]), jnp.sum(total)
    even = at_ref[1] == 0
    values = (jnp.where(even, own, other), jnp.where(even, other, own), jnp.sum(pre_ref[...]))
    tile = pads.shape[2:]
    row = lax.broadcasted_iota(jnp.int32, tile, 0)
    pad = jnp.zeros(tile, F32)
    for i, value in enumerate(values):
        rest = jnp.full(tile, value, F32)
        for n in range(3):
            high = rest.astype(BF16).astype(F32)
            pad = jnp.where(row == 3 * i + n, high, pad)
            rest = rest - high
    pads[...] = jnp.broadcast_to(pad.astype(BF16), pads.shape)
    copy = pltpu.make_async_copy(pads, pieces.at[:, :, :, pl.ds(2 * part, LANES)], out_sems.at[2 * steps])
    copy.start()
    for store in stores + [copy]:
        store.wait()


def late(at, grad, moment, second, own_sq, pre_sq, moment_new, second_new, pieces, steps=4):
    _, rows, size = moment.shape
    state = shape(moment.shape, F32)
    return pl.pallas_call(
        late_kernel,
        in_specs=[SMEM, ANY, ANY, ANY, VMEM, VMEM, ANY, ANY, ANY],
        out_specs=(ANY,) * 3,
        scratch_shapes=[
            pltpu.VMEM(grad.shape, BF16),
            pltpu.VMEM((steps, rows // steps, size), F32),
            pltpu.VMEM((steps, rows // steps, size), F32),
            pltpu.VMEM(pieces.shape[:3] + (LANES,), BF16),
            pltpu.SemaphoreType.DMA((2 * steps + 1,)),
            pltpu.SemaphoreType.DMA((2 * steps + 1,)),
        ],
        out_shape=(state, state, shape(pieces.shape, BF16)),
        input_output_aliases={6: 0, 7: 1, 8: 2},
        compiler_params=params(LATE_LIMIT),
        cost_estimate=cost(15 * rows * size, 20 * rows * size),
        name="other_adam",
    )(at, grad, moment, second, own_sq, pre_sq, moment_new, second_new, pieces)


def add_kernel(at_ref, terms_ref, right_ref, left_ref, _, __, right_out, left_out, terms, stat, sems, out_sems):
    k = 1 - at_ref[1]
    gets = [load(ref.at[k], stat.at[i], sems.at[i]) for i, ref in enumerate((right_ref, left_ref))]
    load(terms_ref, terms, sems.at[2]).wait()
    puts = []
    for i, ref in enumerate((right_out, left_out)):
        gets[i].wait()
        stat[i] = 0.95 * stat[i] + terms[i].astype(F32)
        puts.append(load(stat.at[i], ref.at[k], out_sems.at[i]))
    for copy in puts:
        copy.wait()


def add(at, terms, gram_right, gram_left, right_new, left_new):
    _, rows, size = gram_left.shape
    state = shape(gram_left.shape, F32)
    return pl.pallas_call(
        add_kernel,
        in_specs=[SMEM] + [ANY] * 5,
        out_specs=(ANY, ANY),
        out_shape=(state, state),
        scratch_shapes=[
            pltpu.VMEM((2, rows, size), BF16),
            pltpu.VMEM((2, rows, size), F32),
            pltpu.SemaphoreType.DMA((3,)),
            pltpu.SemaphoreType.DMA((2,)),
        ],
        input_output_aliases={4: 0, 5: 1},
        compiler_params=params(BIG_LIMIT),
        cost_estimate=GRAM_COST,
        name="add_terms",
    )(at, terms, gram_right, gram_left, right_new, left_new)


def finish_kernel(cells, slot_ref, in_ref, out_hbm, ratios, out_ref, sems):
    rows = in_ref.shape[1]
    part = (in_ref.shape[2] - LANES) // 2
    sums = in_ref[:, :, 2 * part :].astype(F32).reshape(-1, REPS, rows, LANES)
    adam_sums = jnp.sum(sums, axis=1)
    for k in range(2):
        adam_all = jnp.sum(adam_sums[:, 3 * k : 3 * k + 3], axis=1, keepdims=True)
        pre_all = jnp.sum((sums[:, k] + sums[:, k + 2])[:, 6:8], axis=1, keepdims=True)
        value = jnp.sqrt(adam_all / cells + 1e-06) / jnp.sqrt(pre_all / cells + 1e-06)
        ratios[:, k] = jnp.broadcast_to(value, (value.shape[0], rows, LANES))

    def place_block(b, _):
        slot = slot_ref[b]
        owner, k = slot // 2, lax.rem(slot, 2)
        by = ratios[owner, k]
        by = jnp.concatenate([by] * (2 * part // LANES), axis=1)
        for n in range(2):
            piece = in_ref[owner * REPS + k + 2 * n, :, : 2 * part].astype(F32) * by
            piece = jnp.concatenate([piece[:, :part], piece[:, part:]], axis=0)
            out_ref[b, 2 * n * rows : 2 * (n + 1) * rows, :] = piece.astype(BF16)
        return 0

    chunk = out_ref.shape[0] // DEALS
    puts = []
    for n in range(DEALS):
        lax.fori_loop(n * chunk, (n + 1) * chunk, place_block, 0, unroll=8)
        part_of = pl.ds(n * chunk, chunk)
        puts.append(load(out_ref.at[part_of], out_hbm.at[part_of], sems.at[n]))
    for copy in puts:
        copy.wait()


def finish(owner_slot, pieces, size):
    count, rows, wide = pieces.shape
    blocks = owner_slot.shape[0]
    part = (wide - LANES) // 2
    return pl.pallas_call(
        functools.partial(finish_kernel, float(size * size)),
        out_shape=shape((blocks, 4 * rows, part), BF16),
        in_specs=[SMEM, VMEM],
        out_specs=ANY,
        scratch_shapes=[
            pltpu.VMEM((blocks // 2, 2, rows, LANES), F32),
            pltpu.VMEM((blocks, 4 * rows, part), BF16),
            pltpu.SemaphoreType.DMA((DEALS,)),
        ],
        compiler_params=params(),
        cost_estimate=cost(8 * blocks * rows * part, 20 * blocks * rows * part),
        name="finish_updates",
    )(owner_slot, pieces)


def per_device(grads, owner_slot, gram_left, gram_right, root_left, root_right, moment, second):
    blocks, row_part, part = grads.shape
    _, rows, size = root_left.shape
    at = place()
    sent = deal(owner_slot, grads)
    keep, ahead, across, back = share_rows(at, root_left, row_part)
    arrived = everyone(sent).reshape(OWNERS, REPS, row_part, part)
    ahead = to_neighbour(ahead)
    across = to_neighbour(across, 2)
    back = to_neighbour(back, -1)

    count = rows // row_part
    other = to_neighbour(lax.dynamic_slice_in_dim(arrived, at[2] * count, count, 0))
    terms, moment_new, second_new, own_sq = near_terms(at, arrived, moment, second)
    arrived, terms = lax.optimization_barrier((arrived, terms))
    terms = to_neighbour(terms)
    pieces, pre_sq = precond(at, arrived, (keep, ahead, across, back), root_right)
    moment_new, second_new, pieces = late(
        at, other, moment, second, own_sq, pre_sq, moment_new, second_new, pieces
    )
    arrived, pieces = lax.optimization_barrier((arrived, pieces))
    homed = everyone(pieces.reshape((-1,) + pieces.shape[2:]))
    left_new, right_new = grams(at, arrived, gram_left, gram_right)
    right_new, left_new = add(at, terms, gram_right, gram_left, right_new, left_new)
    updates = finish(owner_slot, homed, size)
    return (updates, left_new, right_new, moment_new, second_new)


def solution(mesh):
    return jax.shard_map(
        per_device,
        mesh=mesh,
        in_specs=(
            P(None, "fsdp", "rep"),
            P(),
            P("fsdp", "rep", None),
            P("fsdp", "rep", None),
            P("fsdp", "rep", None),
            P("fsdp", None, None),
            P("fsdp", "rep", None),
            P("fsdp", "rep", None),
        ),
        out_specs=(
            P(None, "fsdp", "rep"),
            P("fsdp", "rep", None),
            P("fsdp", "rep", None),
            P("fsdp", "rep", None),
            P("fsdp", "rep", None),
        ),
        check_vma=False,
    )
```

```python
import functools

import jax
import jax.numpy as jnp
from jax import lax
from jax.experimental import pallas as pl
from jax.experimental.pallas import tpu as pltpu
from jax.sharding import PartitionSpec as P

VMEM_LIMIT = 32 * 1024 * 1024
GRAM_LIMIT = 50 * 1024 * 1024
MID_LIMIT = 46 * 1024 * 1024
BIG_LIMIT = 60 * 1024 * 1024
DEALS = 4
LATE_LIMIT = 46 * 1024 * 1024
REPS = 4
OWNERS = 32
LANES = 128
NN = (((1,), (0,)), ((), ()))
NT = (((1,), (1,)), ((), ()))
TN = (((0,), (0,)), ((), ()))
ANY = pl.BlockSpec(memory_space=pl.ANY)
VMEM = pl.BlockSpec(memory_space=pltpu.VMEM)
SMEM = pl.BlockSpec(memory_space=pltpu.SMEM)
BF16 = jnp.bfloat16
F32 = jnp.float32


def params(limit=VMEM_LIMIT):
    return pltpu.CompilerParams(vmem_limit_bytes=limit)


def cost(flops, nbytes):
    return pl.CostEstimate(flops=flops, bytes_accessed=nbytes, transcendentals=0)


def dot(a, b, dims=NN):
    return lax.dot_general(a, b, dims, preferred_element_type=F32)


def shape(dims, dtype):
    return jax.ShapeDtypeStruct(dims, dtype)


GRAM_COST = cost(1, 1)
MID_COST = cost(10**11, 10**6)


def place():
    rep = lax.axis_index("rep").astype(jnp.int32)
    step = 1 - 2 * lax.rem(lax.axis_index("fsdp").astype(jnp.int32), 2)
    return rep, lax.rem(rep, 2), lax.rem(rep + step + REPS, REPS), step


def to_neighbour(x, far=1):
    pairs = []
    for owner in range(OWNERS):
        step = far * (1 - 2 * (owner % 2))
        for rep in range(REPS):
            pairs.append((owner * REPS + rep, owner * REPS + (rep + step) % REPS))
    return lax.ppermute(x, ("fsdp", "rep"), pairs)


def everyone(x):
    return lax.all_to_all(x, ("fsdp", "rep"), split_axis=0, concat_axis=0, tiled=True)


def load(src, dst, sem):
    copy = pltpu.make_async_copy(src, dst, sem)
    copy.start()
    return copy


def deal_kernel(slot_hbm, grads_ref, out_ref, grads, out, slot_ref, block_of, sems):
    blocks = grads.shape[0]
    chunk = blocks // DEALS
    gets, puts = [], []
    get_slots = load(slot_hbm, slot_ref, sems.at[2 * DEALS])
    for n in range(DEALS):
        part_of = pl.ds(n * chunk, chunk)
        gets.append(load(grads_ref.at[part_of], grads.at[part_of], sems.at[n]))

    def note(b, _):
        block_of[slot_ref[b]] = b
        return 0

    get_slots.wait()
    lax.fori_loop(0, blocks, note, 0, unroll=8)
    for copy in gets:
        copy.wait()

    def place_owner(owner, _):
        for k in range(2):
            block = grads[block_of[2 * owner + k]]
            out[owner * REPS + k] = block
            out[owner * REPS + k + 2] = block
        return 0

    step = blocks // 2 // DEALS
    for n in range(DEALS):
        lax.fori_loop(n * step, (n + 1) * step, place_owner, 0, unroll=4)
        part_of = pl.ds(n * step * REPS, step * REPS)
        puts.append(load(out.at[part_of], out_ref.at[part_of], sems.at[DEALS + n]))
    for copy in puts:
        copy.wait()


def deal(owner_slot, grads):
    blocks, row_part, part = grads.shape
    return pl.pallas_call(
        deal_kernel,
        out_shape=shape((2 * blocks, row_part, part), BF16),
        in_specs=[ANY, ANY],
        out_specs=ANY,
        scratch_shapes=[
            pltpu.VMEM(grads.shape, BF16),
            pltpu.VMEM((2 * blocks, row_part, part), BF16),
            pltpu.SMEM((blocks,), jnp.int32),
            pltpu.SMEM((blocks,), jnp.int32),
            pltpu.SemaphoreType.DMA((2 * DEALS + 1,)),
        ],
        compiler_params=params(BIG_LIMIT),
        cost_estimate=cost(0, 6 * grads.size),
        name="deal_blocks",
    )(owner_slot, grads)


def share_kernel(left_ref, ahead_ref, across_ref, back_ref, left, sems, out_sems):
    here = place()
    outs = ((1, ahead_ref), (2, across_ref), (-1, back_ref))
    gets, puts = [], []
    for i, (j, _) in enumerate(outs):
        to = lax.rem(here[0] + j * here[3] + REPS, REPS)
        gets.append(load(left_ref.at[lax.rem(to, 2), :, to // 2], left.at[i], sems.at[i]))
    for i, (_, ref) in enumerate(outs):
        gets[i].wait()
        puts.append(load(left.at[i], ref, out_sems.at[i]))
    for copy in puts:
        copy.wait()


def share_rows(halves):
    _, count, _, half, size = halves.shape
    others = REPS - 1
    return pl.pallas_call(
        share_kernel,
        out_shape=(shape((count, half, size), BF16),) * others,
        in_specs=[ANY],
        out_specs=(ANY,) * others,
        scratch_shapes=[
            pltpu.VMEM((others, count, half, size), BF16),
            pltpu.SemaphoreType.DMA((others,)),
            pltpu.SemaphoreType.DMA((others,)),
        ],
        compiler_params=params(BIG_LIMIT),
        cost_estimate=cost(0, 3 * halves.size),
        name="share_rows",
    )(halves)


def near_kernel(
    g_ref, mom_ref, sec_ref, terms_ref, mom_out, sec_out, sum_ref,
    whole, lhs, terms, mom, sec, sems, out_sems,
):
    here = place()
    rep, k, near = here[0], here[1], here[2]
    owners, reps, row_part, part = g_ref.shape
    size = owners * row_part
    rows = mom.shape[0]
    blocks = rows // row_part
    get_mom = load(mom_ref.at[k], mom, sems.at[0])
    get_sec = load(sec_ref.at[k], sec, sems.at[1])
    puts = []

    def put(src, dst):
        puts.append(load(src, dst, out_sems.at[len(puts)]))

    lhs[...] = g_ref[:, pl.ds(near, 1)].reshape(size, part).T
    for j in range(reps):
        cols = pl.ds(j * part, part)
        terms[0, :, cols] = (0.05 * dot(lhs[...], g_ref[:, j].reshape(size, part))).astype(BF16)
        put(terms.at[0, :, cols], terms_ref.at[0, :, cols])
    for j in range(reps):
        cols = slice(j * part, (j + 1) * part)
        whole[:, cols] = g_ref[:, j].reshape(size, part)
    rows_near = whole[pl.ds(pl.multiple_of(near * rows, rows), rows), :]
    for j in range(reps):
        cols = pl.ds(j * part, part)
        terms[1, :, cols] = (0.05 * dot(rows_near, whole[j * part : (j + 1) * part, :], NT)).astype(BF16)
        put(terms.at[1, :, cols], terms_ref.at[1, :, cols])
    get_mom.wait()
    get_sec.wait()
    total = jnp.zeros((8, part), F32)
    for j in range(reps):
        cols = pl.ds(j * part, part)
        own = g_ref[pl.ds(rep * blocks, blocks), j].reshape(rows, part).astype(F32)
        first = 0.9 * mom[:, cols] + 0.1 * own
        second = 0.95 * sec[:, cols] + 0.05 * own * own
        mom[:, cols] = first
        sec[:, cols] = second
        way = first / (jnp.sqrt(second) + 1e-08)
        total += jnp.sum((way * way).reshape(rows // 8, 8, part), axis=0)
        put(mom.at[:, cols], mom_out.at[k, :, cols])
        put(sec.at[:, cols], sec_out.at[k, :, cols])
    sum_ref[...] = total
    for copy in puts:
        copy.wait()


def near_terms(arrived, moment, second):
    _, reps, _, part = arrived.shape
    _, rows, size = moment.shape
    state = shape(moment.shape, F32)
    return pl.pallas_call(
        near_kernel,
        in_specs=[VMEM, ANY, ANY],
        out_specs=(ANY,) * 3 + (VMEM,),
        scratch_shapes=[
            pltpu.VMEM((size, size), BF16),
            pltpu.VMEM((rows, size), BF16),
            pltpu.VMEM((2, rows, size), BF16),
            pltpu.VMEM((rows, size), F32),
            pltpu.VMEM((rows, size), F32),
            pltpu.SemaphoreType.DMA((2,)),
            pltpu.SemaphoreType.DMA((4 * reps,)),
        ],
        out_shape=(shape((2, rows, size), BF16), state, state, shape((8, part), F32)),
        compiler_params=params(GRAM_LIMIT),
        cost_estimate=GRAM_COST,
        name="near_terms",
    )(arrived, moment, second)


def precond_kernel(
    g_ref, l0_ref, l1_ref, l2_ref, l3_ref, right_ref, pieces, sum_ref, left, right, mixed, out, sems, out_sems
):
    here = place()
    rep, k, step = here[0], here[1], here[3]
    owners, reps, row_part, part = g_ref.shape
    size = owners * row_part
    share = l1_ref.shape[0]
    get_left = []
    for j, ref in enumerate((l0_ref.at[k, :, rep // 2], l1_ref, l2_ref, l3_ref)):
        first = lax.rem(rep - j * step + REPS * REPS, REPS) * share
        get_left.append(load(ref, left.at[pl.ds(first, share)], sems.at[j]))
    half = size // 2
    get_right = [
        load(right_ref.at[k, :, pl.ds(i * half, half)], right.at[:, pl.ds(i * half, half)], sems.at[REPS + i])
        for i in range(2)
    ]
    for copy in get_left:
        copy.wait()
    for j in range(reps):
        grad = g_ref[:, j].reshape(size, part)
        mixed[:, j * part : (j + 1) * part] = dot(left[...].reshape(mixed.shape), grad).astype(BF16)
    for copy in get_right:
        copy.wait()
    total = jnp.zeros((8, part), F32)
    puts = []
    for j in range(reps):
        piece = dot(mixed[...], right[:, j * part : (j + 1) * part])
        total += jnp.sum((piece * piece).reshape(-1, 8, part), axis=0)
        halves = piece.reshape(owners, 2, 8, part)
        for i in range(2):
            out[:, j, :, i * part : (i + 1) * part] = halves[:, i].astype(BF16)
        puts.append(load(out.at[:, j], pieces.at[:, j, :, pl.ds(0, 2 * part)], out_sems.at[j]))
    sum_ref[...] = total
    for copy in puts:
        copy.wait()


def precond(arrived, left_parts, root_right):
    owners, reps, row_part, part = arrived.shape
    size = root_right.shape[1]
    half = row_part // 2
    return pl.pallas_call(
        precond_kernel,
        in_specs=[VMEM] + [ANY] * 5,
        out_specs=(ANY, VMEM),
        scratch_shapes=[
            pltpu.VMEM((owners, half, size), BF16),
            pltpu.VMEM((size, size), BF16),
            pltpu.VMEM((owners * half, size), BF16),
            pltpu.VMEM((owners, reps, half // 2, 2 * part), BF16),
            pltpu.SemaphoreType.DMA((REPS + 2,)),
            pltpu.SemaphoreType.DMA((reps,)),
        ],
        out_shape=(shape((owners, reps, half // 2, 2 * part + LANES), BF16), shape((8, part), F32)),
        compiler_params=params(MID_LIMIT),
        cost_estimate=MID_COST,
        name="precond_rows",
    )(arrived, *left_parts, root_right)


def gram_kernel(arrived, stat_left, stat_right, left_out, right_out, whole, gl, gr, sems, out_sems):
    here = place()
    rep, k = here[0], here[1]
    _, row_part, size = whole.shape
    part = size // REPS
    rows = gl.shape[0]
    blocks = rows // row_part
    columns = [load(arrived.at[:, j], whole.at[:, :, pl.ds(j * part, part)], sems.at[j]) for j in range(REPS)]
    get_gr = load(stat_right.at[k], gr, sems.at[REPS])
    get_gl = load(stat_left.at[k], gl, sems.at[REPS + 1])
    for copy in columns:
        copy.wait()
    grad = whole[...].reshape(size, size)
    own = whole[:, :, pl.ds(pl.multiple_of(rep * part, part), part)].reshape(size, part)
    term = 0.05 * dot(own, grad, TN)
    get_gr.wait()
    gr[...] = 0.95 * gr[...] + term
    put_right = load(gr, right_out.at[k], out_sems.at[0])
    own = whole[pl.ds(rep * blocks, blocks)].reshape(rows, size)
    term = 0.05 * dot(own, grad, NT)
    get_gl.wait()
    gl[...] = 0.95 * gl[...] + term
    put_left = load(gl, left_out.at[k], out_sems.at[1])
    put_right.wait()
    put_left.wait()


def grams(arrived, gram_left, gram_right):
    owners, _, row_part, _ = arrived.shape
    _, rows, size = gram_left.shape
    state = shape(gram_left.shape, F32)
    return pl.pallas_call(
        gram_kernel,
        in_specs=[ANY] * 3,
        out_specs=(ANY,) * 2,
        scratch_shapes=[
            pltpu.VMEM((owners, row_part, size), BF16),
            pltpu.VMEM((rows, size), F32),
            pltpu.VMEM((rows, size), F32),
            pltpu.SemaphoreType.DMA((REPS + 2,)),
            pltpu.SemaphoreType.DMA((2,)),
        ],
        out_shape=(state,) * 2,
        compiler_params=params(BIG_LIMIT),
        cost_estimate=MID_COST,
        name="own_grams",
    )(arrived, gram_left, gram_right)


def late_kernel(
    grad_hbm, mom_ref, sec_ref, own_ref, pre_ref, _, __, ___, mom_out, sec_out, pieces, grad_ref, mom, sec, pads, sems, out_sems
):
    here = place()
    k = 1 - here[1]
    count, reps, row_part, part = grad_ref.shape
    rows = count * row_part
    steps = mom.shape[0]
    chunk = count // steps
    size = reps * part

    def block(ref, n):
        return ref.at[k, pl.ds(n * chunk * row_part, chunk * row_part)]

    get_grad = load(grad_hbm, grad_ref, sems.at[2 * steps])
    loads = []
    for n in range(steps):
        for i, (src, dst) in enumerate(((mom_ref, mom), (sec_ref, sec))):
            copy = pltpu.make_async_copy(block(src, n), dst.at[n], sems.at[2 * n + i])
            copy.start()
            loads.append(copy)
    stores = []
    total = jnp.zeros((8, part), F32)
    get_grad.wait()
    for n in range(steps):
        loads[2 * n].wait()
        loads[2 * n + 1].wait()
        for j in range(reps):
            cols = slice(j * part, (j + 1) * part)
            grad = grad_ref[n * chunk : (n + 1) * chunk, j].reshape(chunk * row_part, part).astype(F32)
            first = 0.9 * mom[n, :, cols] + 0.1 * grad
            second = 0.95 * sec[n, :, cols] + 0.05 * grad * grad
            mom[n, :, cols] = first
            sec[n, :, cols] = second
            way = first / (jnp.sqrt(second) + 1e-08)
            total += jnp.sum((way * way).reshape(-1, 8, part), axis=0)
        for i, (src, dst) in enumerate(((mom, mom_out), (sec, sec_out))):
            copy = pltpu.make_async_copy(src.at[n], block(dst, n), out_sems.at[2 * n + i])
            copy.start()
            stores.append(copy)
    own, other = jnp.sum(own_ref[...]), jnp.sum(total)
    even = here[1] == 0
    values = (jnp.where(even, own, other), jnp.where(even, other, own), jnp.sum(pre_ref[...]))
    tile = pads.shape[2:]
    row = lax.broadcasted_iota(jnp.int32, tile, 0)
    pad = jnp.zeros(tile, F32)
    for i, value in enumerate(values):
        rest = jnp.full(tile, value, F32)
        for n in range(3):
            high = rest.astype(BF16).astype(F32)
            pad = jnp.where(row == 3 * i + n, high, pad)
            rest = rest - high
    pads[...] = jnp.broadcast_to(pad.astype(BF16), pads.shape)
    copy = pltpu.make_async_copy(pads, pieces.at[:, :, :, pl.ds(2 * part, LANES)], out_sems.at[2 * steps])
    copy.start()
    for store in stores + [copy]:
        store.wait()


def late(grad, moment, second, own_sq, pre_sq, moment_new, second_new, pieces, steps=4):
    _, rows, size = moment.shape
    state = shape(moment.shape, F32)
    return pl.pallas_call(
        late_kernel,
        in_specs=[ANY, ANY, ANY, VMEM, VMEM, ANY, ANY, ANY],
        out_specs=(ANY,) * 3,
        scratch_shapes=[
            pltpu.VMEM(grad.shape, BF16),
            pltpu.VMEM((steps, rows // steps, size), F32),
            pltpu.VMEM((steps, rows // steps, size), F32),
            pltpu.VMEM(pieces.shape[:3] + (LANES,), BF16),
            pltpu.SemaphoreType.DMA((2 * steps + 1,)),
            pltpu.SemaphoreType.DMA((2 * steps + 1,)),
        ],
        out_shape=(state, state, shape(pieces.shape, BF16)),
        input_output_aliases={5: 0, 6: 1, 7: 2},
        compiler_params=params(LATE_LIMIT),
        cost_estimate=cost(15 * rows * size, 20 * rows * size),
        name="other_adam",
    )(grad, moment, second, own_sq, pre_sq, moment_new, second_new, pieces)


def add_kernel(terms_ref, right_ref, left_ref, _, __, right_out, left_out, terms, stat, sems, out_sems):
    here = place()
    k = 1 - here[1]
    gets = [load(ref.at[k], stat.at[i], sems.at[i]) for i, ref in enumerate((right_ref, left_ref))]
    load(terms_ref, terms, sems.at[2]).wait()
    puts = []
    for i, ref in enumerate((right_out, left_out)):
        gets[i].wait()
        stat[i] = 0.95 * stat[i] + terms[i].astype(F32)
        puts.append(load(stat.at[i], ref.at[k], out_sems.at[i]))
    for copy in puts:
        copy.wait()


def add(terms, gram_right, gram_left, right_new, left_new):
    _, rows, size = gram_left.shape
    state = shape(gram_left.shape, F32)
    return pl.pallas_call(
        add_kernel,
        in_specs=[ANY] * 5,
        out_specs=(ANY, ANY),
        out_shape=(state, state),
        scratch_shapes=[
            pltpu.VMEM((2, rows, size), BF16),
            pltpu.VMEM((2, rows, size), F32),
            pltpu.SemaphoreType.DMA((3,)),
            pltpu.SemaphoreType.DMA((2,)),
        ],
        input_output_aliases={3: 0, 4: 1},
        compiler_params=params(BIG_LIMIT),
        cost_estimate=GRAM_COST,
        name="add_terms",
    )(terms, gram_right, gram_left, right_new, left_new)


def finish_kernel(cells, slot_ref, in_ref, out_hbm, ratios, out_ref, sems):
    rows = in_ref.shape[1]
    part = (in_ref.shape[2] - LANES) // 2
    sums = in_ref[:, :, 2 * part :].astype(F32).reshape(-1, REPS, rows, LANES)
    adam_sums = jnp.sum(sums, axis=1)
    for k in range(2):
        adam_all = jnp.sum(adam_sums[:, 3 * k : 3 * k + 3], axis=1, keepdims=True)
        pre_all = jnp.sum((sums[:, k] + sums[:, k + 2])[:, 6:8], axis=1, keepdims=True)
        value = jnp.sqrt(adam_all / cells + 1e-06) / jnp.sqrt(pre_all / cells + 1e-06)
        ratios[:, k] = jnp.broadcast_to(value, (value.shape[0], rows, LANES))

    def place_block(b, _):
        slot = slot_ref[b]
        owner, k = slot // 2, lax.rem(slot, 2)
        by = ratios[owner, k]
        by = jnp.concatenate([by] * (2 * part // LANES), axis=1)
        for n in range(2):
            piece = in_ref[owner * REPS + k + 2 * n, :, : 2 * part].astype(F32) * by
            piece = jnp.concatenate([piece[:, :part], piece[:, part:]], axis=0)
            out_ref[b, 2 * n * rows : 2 * (n + 1) * rows, :] = piece.astype(BF16)
        return 0

    chunk = out_ref.shape[0] // DEALS
    puts = []
    for n in range(DEALS):
        lax.fori_loop(n * chunk, (n + 1) * chunk, place_block, 0, unroll=16)
        part_of = pl.ds(n * chunk, chunk)
        puts.append(load(out_ref.at[part_of], out_hbm.at[part_of], sems.at[n]))
    for copy in puts:
        copy.wait()


def finish(owner_slot, pieces, size):
    count, rows, wide = pieces.shape
    blocks = owner_slot.shape[0]
    part = (wide - LANES) // 2
    return pl.pallas_call(
        functools.partial(finish_kernel, float(size * size)),
        out_shape=shape((blocks, 4 * rows, part), BF16),
        in_specs=[SMEM, VMEM],
        out_specs=ANY,
        scratch_shapes=[
            pltpu.VMEM((blocks // 2, 2, rows, LANES), F32),
            pltpu.VMEM((blocks, 4 * rows, part), BF16),
            pltpu.SemaphoreType.DMA((DEALS,)),
        ],
        compiler_params=params(),
        cost_estimate=cost(8 * blocks * rows * part, 20 * blocks * rows * part),
        name="finish_updates",
    )(owner_slot, pieces)


def per_device(grads, owner_slot, gram_left, gram_right, root_left, root_right, moment, second):
    blocks, row_part, part = grads.shape
    _, rows, size = root_left.shape
    near = place()[2]
    sent = deal(owner_slot, grads)
    halves = root_left.reshape(2, rows // row_part, 2, row_part // 2, size)
    ahead, across, back = share_rows(halves)
    arrived = everyone(sent).reshape(OWNERS, REPS, row_part, part)
    ahead = to_neighbour(ahead)
    across = to_neighbour(across, 2)
    back = to_neighbour(back, -1)

    count = rows // row_part
    other = to_neighbour(lax.dynamic_slice_in_dim(arrived, near * count, count, 0))
    terms, moment_new, second_new, own_sq = near_terms(arrived, moment, second)
    arrived, terms = lax.optimization_barrier((arrived, terms))
    terms = to_neighbour(terms)
    pieces, pre_sq = precond(arrived, (halves, ahead, across, back), root_right)
    moment_new, second_new, pieces = late(
        other, moment, second, own_sq, pre_sq, moment_new, second_new, pieces
    )
    arrived, pieces = lax.optimization_barrier((arrived, pieces))
    homed = everyone(pieces.reshape((-1,) + pieces.shape[2:]))
    left_new, right_new = grams(arrived, gram_left, gram_right)
    right_new, left_new = add(terms, gram_right, gram_left, right_new, left_new)
    updates = finish(owner_slot, homed, size)
    return (updates, left_new, right_new, moment_new, second_new)


def solution(mesh):
    return jax.shard_map(
        per_device,
        mesh=mesh,
        in_specs=(
            P(None, "fsdp", "rep"),
            P(),
            P("fsdp", "rep", None),
            P("fsdp", "rep", None),
            P("fsdp", "rep", None),
            P("fsdp", None, None),
            P("fsdp", "rep", None),
            P("fsdp", "rep", None),
        ),
        out_specs=(
            P(None, "fsdp", "rep"),
            P("fsdp", "rep", None),
            P("fsdp", "rep", None),
            P("fsdp", "rep", None),
            P("fsdp", "rep", None),
        ),
        check_vma=False,
    )
```

```python
import functools

import jax
import jax.numpy as jnp
from jax import lax
from jax.experimental import pallas as pl
from jax.experimental.pallas import tpu as pltpu
from jax.sharding import PartitionSpec as P

VMEM_LIMIT = 32 * 1024 * 1024
GRAM_LIMIT = 46 * 1024 * 1024
MID_LIMIT = 46 * 1024 * 1024
BIG_LIMIT = 60 * 1024 * 1024
DEALS = 4
LATE_LIMIT = 46 * 1024 * 1024
REPS = 4
OWNERS = 32
LANES = 128
NN = (((1,), (0,)), ((), ()))
NT = (((1,), (1,)), ((), ()))
TN = (((0,), (0,)), ((), ()))
ANY = pl.BlockSpec(memory_space=pl.ANY)
VMEM = pl.BlockSpec(memory_space=pltpu.VMEM)
SMEM = pl.BlockSpec(memory_space=pltpu.SMEM)
BF16 = jnp.bfloat16
F32 = jnp.float32


def params(limit=VMEM_LIMIT):
    return pltpu.CompilerParams(vmem_limit_bytes=limit)


def cost(flops, nbytes):
    return pl.CostEstimate(flops=flops, bytes_accessed=nbytes, transcendentals=0)


def dot(a, b, dims=NN):
    return lax.dot_general(a, b, dims, preferred_element_type=F32)


def shape(dims, dtype):
    return jax.ShapeDtypeStruct(dims, dtype)


GRAM_COST = cost(1, 1)
MID_COST = cost(10**11, 10**6)


def place():
    rep = lax.axis_index("rep").astype(jnp.int32)
    step = 1 - 2 * lax.rem(lax.axis_index("fsdp").astype(jnp.int32), 2)
    return rep, lax.rem(rep, 2), lax.rem(rep + step + REPS, REPS), step


def to_neighbour(x, far=1):
    pairs = []
    for owner in range(OWNERS):
        step = far * (1 - 2 * (owner % 2))
        for rep in range(REPS):
            pairs.append((owner * REPS + rep, owner * REPS + (rep + step) % REPS))
    return lax.ppermute(x, ("fsdp", "rep"), pairs)


def everyone(x):
    return lax.all_to_all(x, ("fsdp", "rep"), split_axis=0, concat_axis=0, tiled=True)


def load(src, dst, sem):
    copy = pltpu.make_async_copy(src, dst, sem)
    copy.start()
    return copy


def deal_kernel(slot_hbm, grads_ref, out_ref, grads, out, slot_ref, block_of, sems):
    blocks = grads.shape[0]
    chunk = blocks // DEALS
    gets, puts = [], []
    get_slots = load(slot_hbm, slot_ref, sems.at[2 * DEALS])
    for n in range(DEALS):
        part_of = pl.ds(n * chunk, chunk)
        gets.append(load(grads_ref.at[part_of], grads.at[part_of], sems.at[n]))

    def note(b, _):
        block_of[slot_ref[b]] = b
        return 0

    get_slots.wait()
    lax.fori_loop(0, blocks, note, 0, unroll=8)
    for copy in gets:
        copy.wait()

    def place_owner(owner, _):
        for k in range(2):
            block = grads[block_of[2 * owner + k]]
            out[owner * REPS + k] = block
            out[owner * REPS + k + 2] = block
        return 0

    step = blocks // 2 // DEALS
    for n in range(DEALS):
        lax.fori_loop(n * step, (n + 1) * step, place_owner, 0, unroll=4)
        part_of = pl.ds(n * step * REPS, step * REPS)
        puts.append(load(out.at[part_of], out_ref.at[part_of], sems.at[DEALS + n]))
    for copy in puts:
        copy.wait()


def deal(owner_slot, grads):
    blocks, row_part, part = grads.shape
    return pl.pallas_call(
        deal_kernel,
        out_shape=shape((2 * blocks, row_part, part), BF16),
        in_specs=[ANY, ANY],
        out_specs=ANY,
        scratch_shapes=[
            pltpu.VMEM(grads.shape, BF16),
            pltpu.VMEM((2 * blocks, row_part, part), BF16),
            pltpu.SMEM((blocks,), jnp.int32),
            pltpu.SMEM((blocks,), jnp.int32),
            pltpu.SemaphoreType.DMA((2 * DEALS + 1,)),
        ],
        compiler_params=params(BIG_LIMIT),
        cost_estimate=cost(0, 6 * grads.size),
        name="deal_blocks",
    )(owner_slot, grads)


def share_kernel(left_ref, ahead_ref, across_ref, back_ref, left, sems, out_sems):
    here = place()
    outs = ((1, ahead_ref), (2, across_ref), (-1, back_ref))
    gets, puts = [], []
    for i, (j, _) in enumerate(outs):
        to = lax.rem(here[0] + j * here[3] + REPS, REPS)
        gets.append(load(left_ref.at[lax.rem(to, 2), :, to // 2], left.at[i], sems.at[i]))
    for i, (_, ref) in enumerate(outs):
        gets[i].wait()
        puts.append(load(left.at[i], ref, out_sems.at[i]))
    for copy in puts:
        copy.wait()


def share_rows(halves):
    _, count, _, half, size = halves.shape
    others = REPS - 1
    return pl.pallas_call(
        share_kernel,
        out_shape=(shape((count, half, size), BF16),) * others,
        in_specs=[ANY],
        out_specs=(ANY,) * others,
        scratch_shapes=[
            pltpu.VMEM((others, count, half, size), BF16),
            pltpu.SemaphoreType.DMA((others,)),
            pltpu.SemaphoreType.DMA((others,)),
        ],
        compiler_params=params(BIG_LIMIT),
        cost_estimate=cost(0, 3 * halves.size),
        name="share_rows",
    )(halves)


def near_kernel(
    g_ref, mom_ref, sec_ref, terms_ref, mom_out, sec_out, sum_ref,
    whole, lhs, terms, mom, sec, total_ref, sems, out_sems,
):
    here = place()
    rep, k, near = here[0], here[1], here[2]
    owners, reps, row_part, part = g_ref.shape
    size = owners * row_part
    rows = mom.shape[0]
    blocks = rows // row_part
    get_mom = load(mom_ref.at[k], mom, sems.at[0])
    get_sec = load(sec_ref.at[k], sec, sems.at[1])
    puts = []

    def put(src, dst):
        puts.append(load(src, dst, out_sems.at[len(puts)]))

    lhs[...] = g_ref[:, pl.ds(near, 1)].reshape(size, part).T
    for j in range(reps):
        cols = pl.ds(j * part, part)
        terms[0, :, cols] = (0.05 * dot(lhs[...], g_ref[:, j].reshape(size, part))).astype(BF16)
        put(terms.at[0, :, cols], terms_ref.at[0, :, cols])
    for j in range(reps):
        cols = slice(j * part, (j + 1) * part)
        whole[:, cols] = g_ref[:, j].reshape(size, part)
    rows_near = whole[pl.ds(pl.multiple_of(near * rows, rows), rows), :]
    for j in range(reps):
        cols = pl.ds(j * part, part)
        terms[1, :, cols] = (0.05 * dot(rows_near, whole[j * part : (j + 1) * part, :], NT)).astype(BF16)
        put(terms.at[1, :, cols], terms_ref.at[1, :, cols])
    get_mom.wait()
    get_sec.wait()
    total = jnp.zeros((8, part), F32)
    for j in range(reps):
        cols = pl.ds(j * part, part)
        own = g_ref[pl.ds(rep * blocks, blocks), j].reshape(rows, part).astype(F32)
        first = 0.9 * mom[:, cols] + 0.1 * own
        second = 0.95 * sec[:, cols] + 0.05 * own * own
        mom[:, cols] = first
        sec[:, cols] = second
        way = first / (jnp.sqrt(second) + 1e-08)
        total += jnp.sum((way * way).reshape(rows // 8, 8, part), axis=0)
        put(mom.at[:, cols], mom_out.at[k, :, cols])
        put(sec.at[:, cols], sec_out.at[k, :, cols])
    total_ref[...] = total
    put(total_ref, sum_ref)
    for copy in puts:
        copy.wait()


def near_terms(arrived, moment, second):
    _, reps, _, part = arrived.shape
    _, rows, size = moment.shape
    state = shape(moment.shape, F32)
    return pl.pallas_call(
        near_kernel,
        in_specs=[VMEM, ANY, ANY],
        out_specs=(ANY,) * 4,
        scratch_shapes=[
            pltpu.VMEM((size, size), BF16),
            pltpu.VMEM((rows, size), BF16),
            pltpu.VMEM((2, rows, size), BF16),
            pltpu.VMEM((rows, size), F32),
            pltpu.VMEM((rows, size), F32),
            pltpu.VMEM((8, part), F32),
            pltpu.SemaphoreType.DMA((2,)),
            pltpu.SemaphoreType.DMA((4 * reps + 1,)),
        ],
        out_shape=(shape((2, rows, size), BF16), state, state, shape((8, part), F32)),
        compiler_params=params(GRAM_LIMIT),
        cost_estimate=GRAM_COST,
        name="near_terms",
    )(arrived, moment, second)


def precond_kernel(
    g_ref, l0_ref, l1_ref, l2_ref, l3_ref, right_ref, pieces, sum_ref, left, right, mixed, out, total_ref, sems, out_sems
):
    here = place()
    rep, k, step = here[0], here[1], here[3]
    owners, reps, row_part, part = g_ref.shape
    size = owners * row_part
    share = l1_ref.shape[0]
    get_left = []
    for j, ref in enumerate((l0_ref.at[k, :, rep // 2], l1_ref, l2_ref, l3_ref)):
        first = lax.rem(rep - j * step + REPS * REPS, REPS) * share
        get_left.append(load(ref, left.at[pl.ds(first, share)], sems.at[j]))
    half = size // 2
    get_right = [
        load(right_ref.at[k, :, pl.ds(i * half, half)], right.at[:, pl.ds(i * half, half)], sems.at[REPS + i])
        for i in range(2)
    ]
    for copy in get_left:
        copy.wait()
    for j in range(reps):
        grad = g_ref[:, j].reshape(size, part)
        mixed[:, j * part : (j + 1) * part] = dot(left[...].reshape(mixed.shape), grad).astype(BF16)
    for copy in get_right:
        copy.wait()
    total = jnp.zeros((8, part), F32)
    puts = []
    for j in range(reps):
        piece = dot(mixed[...], right[:, j * part : (j + 1) * part])
        total += jnp.sum((piece * piece).reshape(-1, 8, part), axis=0)
        halves = piece.reshape(owners, 2, 8, part)
        for i in range(2):
            out[:, j, :, i * part : (i + 1) * part] = halves[:, i].astype(BF16)
        puts.append(load(out.at[:, j], pieces.at[:, j, :, pl.ds(0, 2 * part)], out_sems.at[j]))
    total_ref[...] = total
    puts.append(load(total_ref, sum_ref, out_sems.at[reps]))
    for copy in puts:
        copy.wait()


def precond(arrived, left_parts, root_right):
    owners, reps, row_part, part = arrived.shape
    size = root_right.shape[1]
    half = row_part // 2
    return pl.pallas_call(
        precond_kernel,
        in_specs=[VMEM] + [ANY] * 5,
        out_specs=(ANY, ANY),
        scratch_shapes=[
            pltpu.VMEM((owners, half, size), BF16),
            pltpu.VMEM((size, size), BF16),
            pltpu.VMEM((owners * half, size), BF16),
            pltpu.VMEM((owners, reps, half // 2, 2 * part), BF16),
            pltpu.VMEM((8, part), F32),
            pltpu.SemaphoreType.DMA((REPS + 2,)),
            pltpu.SemaphoreType.DMA((reps + 1,)),
        ],
        out_shape=(shape((owners, reps, half // 2, 2 * part + LANES), BF16), shape((8, part), F32)),
        compiler_params=params(MID_LIMIT),
        cost_estimate=MID_COST,
        name="precond_rows",
    )(arrived, *left_parts, root_right)


def gram_kernel(arrived, stat_left, stat_right, left_out, right_out, whole, gl, gr, sems, out_sems):
    here = place()
    rep, k = here[0], here[1]
    _, row_part, size = whole.shape
    part = size // REPS
    rows = gl.shape[0]
    blocks = rows // row_part
    columns = [load(arrived.at[:, j], whole.at[:, :, pl.ds(j * part, part)], sems.at[j]) for j in range(REPS)]
    get_gr = load(stat_right.at[k], gr, sems.at[REPS])
    get_gl = load(stat_left.at[k], gl, sems.at[REPS + 1])
    for copy in columns:
        copy.wait()
    grad = whole[...].reshape(size, size)
    own = whole[:, :, pl.ds(pl.multiple_of(rep * part, part), part)].reshape(size, part)
    term = 0.05 * dot(own, grad, TN)
    get_gr.wait()
    gr[...] = 0.95 * gr[...] + term
    put_right = load(gr, right_out.at[k], out_sems.at[0])
    own = whole[pl.ds(rep * blocks, blocks)].reshape(rows, size)
    term = 0.05 * dot(own, grad, NT)
    get_gl.wait()
    gl[...] = 0.95 * gl[...] + term
    put_left = load(gl, left_out.at[k], out_sems.at[1])
    put_right.wait()
    put_left.wait()


def grams(arrived, gram_left, gram_right):
    owners, _, row_part, _ = arrived.shape
    _, rows, size = gram_left.shape
    state = shape(gram_left.shape, F32)
    return pl.pallas_call(
        gram_kernel,
        in_specs=[ANY] * 3,
        out_specs=(ANY,) * 2,
        scratch_shapes=[
            pltpu.VMEM((owners, row_part, size), BF16),
            pltpu.VMEM((rows, size), F32),
            pltpu.VMEM((rows, size), F32),
            pltpu.SemaphoreType.DMA((REPS + 2,)),
            pltpu.SemaphoreType.DMA((2,)),
        ],
        out_shape=(state,) * 2,
        compiler_params=params(BIG_LIMIT),
        cost_estimate=MID_COST,
        name="own_grams",
    )(arrived, gram_left, gram_right)


def late_kernel(
    grad_hbm, mom_ref, sec_ref, own_hbm, pre_hbm, _, __, ___, mom_out, sec_out, pieces, grad_ref, mom, sec, pads, own_ref, pre_ref, sems, out_sems
):
    here = place()
    k = 1 - here[1]
    count, reps, row_part, part = grad_ref.shape
    rows = count * row_part
    steps = mom.shape[0]
    chunk = count // steps
    size = reps * part

    def block(ref, n):
        return ref.at[k, pl.ds(n * chunk * row_part, chunk * row_part)]

    get_grad = load(grad_hbm, grad_ref, sems.at[2 * steps])
    get_sums = [
        load(own_hbm, own_ref, sems.at[2 * steps + 1]),
        load(pre_hbm, pre_ref, sems.at[2 * steps + 2]),
    ]
    loads = []
    for n in range(steps):
        for i, (src, dst) in enumerate(((mom_ref, mom), (sec_ref, sec))):
            copy = pltpu.make_async_copy(block(src, n), dst.at[n], sems.at[2 * n + i])
            copy.start()
            loads.append(copy)
    stores = []
    total = jnp.zeros((8, part), F32)
    get_grad.wait()
    for n in range(steps):
        loads[2 * n].wait()
        loads[2 * n + 1].wait()
        for j in range(reps):
            cols = slice(j * part, (j + 1) * part)
            grad = grad_ref[n * chunk : (n + 1) * chunk, j].reshape(chunk * row_part, part).astype(F32)
            first = 0.9 * mom[n, :, cols] + 0.1 * grad
            second = 0.95 * sec[n, :, cols] + 0.05 * grad * grad
            mom[n, :, cols] = first
            sec[n, :, cols] = second
            way = first / (jnp.sqrt(second) + 1e-08)
            total += jnp.sum((way * way).reshape(-1, 8, part), axis=0)
        for i, (src, dst) in enumerate(((mom, mom_out), (sec, sec_out))):
            copy = pltpu.make_async_copy(src.at[n], block(dst, n), out_sems.at[2 * n + i])
            copy.start()
            stores.append(copy)
    for copy in get_sums:
        copy.wait()
    own, other = jnp.sum(own_ref[...]), jnp.sum(total)
    even = here[1] == 0
    values = (jnp.where(even, own, other), jnp.where(even, other, own), jnp.sum(pre_ref[...]))
    tile = pads.shape[2:]
    row = lax.broadcasted_iota(jnp.int32, tile, 0)
    pad = jnp.zeros(tile, F32)
    for i, value in enumerate(values):
        rest = jnp.full(tile, value, F32)
        for n in range(3):
            high = rest.astype(BF16).astype(F32)
            pad = jnp.where(row == 3 * i + n, high, pad)
            rest = rest - high
    pads[...] = jnp.broadcast_to(pad.astype(BF16), pads.shape)
    copy = pltpu.make_async_copy(pads, pieces.at[:, :, :, pl.ds(2 * part, LANES)], out_sems.at[2 * steps])
    copy.start()
    for store in stores + [copy]:
        store.wait()


def late(grad, moment, second, own_sq, pre_sq, moment_new, second_new, pieces, steps=4):
    _, rows, size = moment.shape
    state = shape(moment.shape, F32)
    return pl.pallas_call(
        late_kernel,
        in_specs=[ANY] * 8,
        out_specs=(ANY,) * 3,
        scratch_shapes=[
            pltpu.VMEM(grad.shape, BF16),
            pltpu.VMEM((steps, rows // steps, size), F32),
            pltpu.VMEM((steps, rows // steps, size), F32),
            pltpu.VMEM(pieces.shape[:3] + (LANES,), BF16),
            pltpu.VMEM(own_sq.shape, F32),
            pltpu.VMEM(pre_sq.shape, F32),
            pltpu.SemaphoreType.DMA((2 * steps + 3,)),
            pltpu.SemaphoreType.DMA((2 * steps + 1,)),
        ],
        out_shape=(state, state, shape(pieces.shape, BF16)),
        input_output_aliases={5: 0, 6: 1, 7: 2},
        compiler_params=params(LATE_LIMIT),
        cost_estimate=cost(15 * rows * size, 20 * rows * size),
        name="other_adam",
    )(grad, moment, second, own_sq, pre_sq, moment_new, second_new, pieces)


def add_kernel(terms_ref, right_ref, left_ref, _, __, right_out, left_out, terms, stat, sems, out_sems):
    here = place()
    k = 1 - here[1]
    gets = [load(ref.at[k], stat.at[i], sems.at[i]) for i, ref in enumerate((right_ref, left_ref))]
    load(terms_ref, terms, sems.at[2]).wait()
    puts = []
    for i, ref in enumerate((right_out, left_out)):
        gets[i].wait()
        stat[i] = 0.95 * stat[i] + terms[i].astype(F32)
        puts.append(load(stat.at[i], ref.at[k], out_sems.at[i]))
    for copy in puts:
        copy.wait()


def add(terms, gram_right, gram_left, right_new, left_new):
    _, rows, size = gram_left.shape
    state = shape(gram_left.shape, F32)
    return pl.pallas_call(
        add_kernel,
        in_specs=[ANY] * 5,
        out_specs=(ANY, ANY),
        out_shape=(state, state),
        scratch_shapes=[
            pltpu.VMEM((2, rows, size), BF16),
            pltpu.VMEM((2, rows, size), F32),
            pltpu.SemaphoreType.DMA((3,)),
            pltpu.SemaphoreType.DMA((2,)),
        ],
        input_output_aliases={3: 0, 4: 1},
        compiler_params=params(BIG_LIMIT),
        cost_estimate=GRAM_COST,
        name="add_terms",
    )(terms, gram_right, gram_left, right_new, left_new)


def finish_kernel(cells, slot_hbm, in_ref, out_hbm, ratios, out_ref, slot_ref, sems):
    get_slots = load(slot_hbm, slot_ref, sems.at[DEALS])
    rows = in_ref.shape[1]
    part = (in_ref.shape[2] - LANES) // 2
    sums = in_ref[:, :, 2 * part :].astype(F32).reshape(-1, REPS, rows, LANES)
    adam_sums = jnp.sum(sums, axis=1)
    for k in range(2):
        adam_all = jnp.sum(adam_sums[:, 3 * k : 3 * k + 3], axis=1, keepdims=True)
        pre_all = jnp.sum((sums[:, k] + sums[:, k + 2])[:, 6:8], axis=1, keepdims=True)
        value = jnp.sqrt(adam_all / cells + 1e-06) / jnp.sqrt(pre_all / cells + 1e-06)
        ratios[:, k] = jnp.broadcast_to(value, (value.shape[0], rows, LANES))

    def place_block(b, _):
        slot = slot_ref[b]
        owner, k = slot // 2, lax.rem(slot, 2)
        by = ratios[owner, k]
        by = jnp.concatenate([by] * (2 * part // LANES), axis=1)
        for n in range(2):
            piece = in_ref[owner * REPS + k + 2 * n, :, : 2 * part].astype(F32) * by
            piece = jnp.concatenate([piece[:, :part], piece[:, part:]], axis=0)
            out_ref[b, 2 * n * rows : 2 * (n + 1) * rows, :] = piece.astype(BF16)
        return 0

    chunk = out_ref.shape[0] // DEALS
    puts = []
    get_slots.wait()
    for n in range(DEALS):
        lax.fori_loop(n * chunk, (n + 1) * chunk, place_block, 0, unroll=16)
        part_of = pl.ds(n * chunk, chunk)
        puts.append(load(out_ref.at[part_of], out_hbm.at[part_of], sems.at[n]))
    for copy in puts:
        copy.wait()


def finish(owner_slot, pieces, size):
    count, rows, wide = pieces.shape
    blocks = owner_slot.shape[0]
    part = (wide - LANES) // 2
    return pl.pallas_call(
        functools.partial(finish_kernel, float(size * size)),
        out_shape=shape((blocks, 4 * rows, part), BF16),
        in_specs=[ANY, VMEM],
        out_specs=ANY,
        scratch_shapes=[
            pltpu.VMEM((blocks // 2, 2, rows, LANES), F32),
            pltpu.VMEM((blocks, 4 * rows, part), BF16),
            pltpu.SMEM((blocks,), jnp.int32),
            pltpu.SemaphoreType.DMA((DEALS + 1,)),
        ],
        compiler_params=params(),
        cost_estimate=cost(8 * blocks * rows * part, 20 * blocks * rows * part),
        name="finish_updates",
    )(owner_slot, pieces)


def per_device(grads, owner_slot, gram_left, gram_right, root_left, root_right, moment, second):
    blocks, row_part, part = grads.shape
    _, rows, size = root_left.shape
    near = place()[2]
    sent = deal(owner_slot, grads)
    halves = root_left.reshape(2, rows // row_part, 2, row_part // 2, size)
    ahead, across, back = share_rows(halves)
    arrived = everyone(sent).reshape(OWNERS, REPS, row_part, part)
    ahead = to_neighbour(ahead)
    across = to_neighbour(across, 2)
    back = to_neighbour(back, -1)

    count = rows // row_part
    other = to_neighbour(lax.dynamic_slice_in_dim(arrived, near * count, count, 0))
    terms, moment_new, second_new, own_sq = near_terms(arrived, moment, second)
    arrived, terms = lax.optimization_barrier((arrived, terms))
    terms = to_neighbour(terms)
    pieces, pre_sq = precond(arrived, (halves, ahead, across, back), root_right)
    moment_new, second_new, pieces = late(
        other, moment, second, own_sq, pre_sq, moment_new, second_new, pieces
    )
    arrived, pieces = lax.optimization_barrier((arrived, pieces))
    homed = everyone(pieces.reshape((-1,) + pieces.shape[2:]))
    left_new, right_new = grams(arrived, gram_left, gram_right)
    right_new, left_new = add(terms, gram_right, gram_left, right_new, left_new)
    updates = finish(owner_slot, homed, size)
    return (updates, left_new, right_new, moment_new, second_new)


def solution(mesh):
    return jax.shard_map(
        per_device,
        mesh=mesh,
        in_specs=(
            P(None, "fsdp", "rep"),
            P(),
            P("fsdp", "rep", None),
            P("fsdp", "rep", None),
            P("fsdp", "rep", None),
            P("fsdp", None, None),
            P("fsdp", "rep", None),
            P("fsdp", "rep", None),
        ),
        out_specs=(
            P(None, "fsdp", "rep"),
            P("fsdp", "rep", None),
            P("fsdp", "rep", None),
            P("fsdp", "rep", None),
            P("fsdp", "rep", None),
        ),
        check_vma=False,
    )
```
